512 devices in a mesh: batch: 32 (over z, y_hi, core), row: 4 (over y_lo), col: 4 (over x).
Axes of the slice: x: 4, y: 8 (y_hi: 2, y_lo: 4; y = y_hi * 4 + y_lo), z: 8, core: 2. Of those that a mesh axis runs over, the one named last changes fastest.
Arguments:
- view_a: bfloat16 [8192, 4096], P('batch', 'row'), may hold values from -1100 to 1100
- view_b: bfloat16 [8192, 4096], P('batch', 'col'), may hold values from -1100 to 1100
Outputs:
- grad_view_a: float32 [8192, 4096], P('batch', 'row')
- grad_view_b: float32 [8192, 4096], P('batch', 'col')
- loss_value: float32 [], replicated
The draws below stay inside these ranges and needn't reach their ends.
All inputs are finite; a program needn't handle non-finite values.
Results may differ from the reference program's by a relative error of at most 0.0053.
Values may be sent and summed in bfloat16 or wider, within the bound.
A program may use at most 64 MiB of HBM per device.

```python
import math
import jax
import jax.numpy as jnp
from jax import lax

FEAT = 4096
SAMPLES = 8192


load_count = 8


def shared_parts(key, load_size):
    key_base, key_factor, key_index, key_load, key_rows = jax.random.split(key, 5)
    baseline = 0.5 * jnp.clip(jax.random.normal(key_base, (SAMPLES, FEAT), jnp.float32), -4.0, 4.0)
    factors = jnp.clip(jax.random.normal(key_factor, (SAMPLES, FEAT // 4), jnp.float32), -4.0, 4.0)
    chosen = jax.random.randint(key_index, (FEAT, load_count), 0, FEAT // 4)
    loadings = jnp.clip(jax.random.normal(key_load, (FEAT, load_count), jnp.float32), -2.0, 2.0)
    loadings = loadings * (load_size / math.sqrt(load_count))
    signal = baseline
    for position in range(load_count):
        signal = signal + loadings[:, position][None, :] * jnp.take(factors, chosen[:, position], axis=1)
    rising = jnp.exp(math.log(3.0) * jnp.arange(SAMPLES, dtype=jnp.float32) / SAMPLES)
    row_scale = jnp.exp(jax.random.uniform(key_rows, (SAMPLES,), jnp.float32, 0.0, math.log(3.0))) * rising
    return (signal, row_scale)


def make_view(shared, key, noise_lo, noise_hi, mean_size):
    signal, row_scale = shared
    key_own, key_noise, key_cols, key_mean = jax.random.split(key, 4)
    private = jnp.clip(jax.random.normal(key_own, (SAMPLES, FEAT), jnp.float32), -4.0, 4.0)
    noise_scale = jnp.exp(jax.random.uniform(key_noise, (FEAT,), jnp.float32, math.log(noise_lo), math.log(noise_hi)))
    col_scale = jnp.exp(jax.random.uniform(key_cols, (FEAT,), jnp.float32, 0.0, math.log(10.0)))
    offset = jax.random.uniform(key_mean, (FEAT,), jnp.float32, -mean_size, mean_size)
    mixed = jnp.clip(signal + noise_scale[None, :] * private, -12.0, 12.0)
    return (col_scale[None, :] * (row_scale[:, None] * mixed + offset[None, :])).astype(jnp.bfloat16)


def draw_view_a(key, part):
    shared = shared_parts(key, 1.0)
    key = jax.random.fold_in(key, 11)
    return make_view(shared, key, 0.15, 0.6, 0.5)


def draw_view_b(key, part):
    shared = shared_parts(key, 1.0)
    key = jax.random.fold_in(key, 23)
    return make_view(shared, key, 0.15, 0.6, 0.5)


def setup_inputs(seed: int = 0) -> dict:
    key_of = jax.random.split(jax.random.key(seed), 3)
    return {
        "view_a": draw_view_a(jax.random.fold_in(key_of[2], 71), 0),
        "view_b": draw_view_b(jax.random.fold_in(key_of[2], 71), 0),
    }


EPSILON = 1e-05
LAMBDA_OFF = 0.0051

def reference(view_a, view_b):
    wide_a = view_a.astype(jnp.float32)
    wide_b = view_b.astype(jnp.float32)
    mean_a = lax.optimization_barrier(jnp.sum(wide_a, axis=0)) / SAMPLES
    mean_b = lax.optimization_barrier(jnp.sum(wide_b, axis=0)) / SAMPLES
    inv_a = lax.rsqrt(lax.optimization_barrier(jnp.sum(wide_a * wide_a, axis=0)) / SAMPLES - mean_a * mean_a + EPSILON)
    inv_b = lax.rsqrt(lax.optimization_barrier(jnp.sum(wide_b * wide_b, axis=0)) / SAMPLES - mean_b * mean_b + EPSILON)
    gram = jnp.dot(wide_a.T, wide_b, preferred_element_type=jnp.float32)
    correl = (gram / SAMPLES - mean_a[:, None] * mean_b[None, :]) * (inv_a[:, None] * inv_b[None, :])
    feat_ids = lax.iota(jnp.int32, FEAT)
    on_diag = feat_ids[:, None] == feat_ids[None, :]
    slope = jnp.where(on_diag, -2.0 * (1.0 - correl), 2.0 * LAMBDA_OFF * correl)
    penalty = jnp.sum(jnp.where(on_diag, jnp.square(1.0 - correl), LAMBDA_OFF * jnp.square(correl)))
    loss_value = penalty / FEAT
    scaled = (slope * (inv_a[:, None] * inv_b[None, :])).astype(jnp.bfloat16)
    scaled_wide = lax.optimization_barrier(scaled).astype(jnp.float32)
    weighted = slope * correl
    row_terms = lax.optimization_barrier(jnp.sum(weighted, axis=1))
    col_terms = lax.optimization_barrier(jnp.sum(weighted, axis=0))
    back_a = jnp.dot(wide_b, scaled_wide.T, preferred_element_type=jnp.float32)
    back_b = jnp.dot(wide_a, scaled_wide, preferred_element_type=jnp.float32)
    shift_a = jnp.dot(scaled_wide, mean_b, precision=lax.Precision.HIGHEST)
    shift_b = jnp.dot(mean_a, scaled_wide, precision=lax.Precision.HIGHEST)
    grad_view_a = back_a - shift_a[None, :] - (inv_a * inv_a * row_terms)[None, :] * (wide_a - mean_a[None, :])
    grad_view_b = back_b - shift_b[None, :] - (inv_b * inv_b * col_terms)[None, :] * (wide_b - mean_b[None, :])
    return (grad_view_a, grad_view_b, loss_value)
```

```python
import functools

import jax
import jax.numpy as jnp
from jax import lax
from jax.experimental import pallas as pl
from jax.experimental.pallas import tpu as pltpu
from jax.sharding import PartitionSpec as P

EPSILON = 1e-05
LAMBDA_OFF = 0.0051
MESH = pl.DeviceIdType.MESH
F32, BF16 = jnp.float32, jnp.bfloat16
NC = 2
NDMA = 160


def kernel(cfg, a_ref, b_ref, oa_ref, ob_ref, loss_ref,
           ax, bx, st_loc, st_sib, st_chip, st_rs, st_zs, st_yin, st, vec,
           h, rx, rx0, hy, hyin, sh, gb, gbrs, gbt, ga, gars, gat, rtv, sav, ls, lx, ly,
           send_sem, recv_sem):
    NZ, YH, NX, NY, S, F, N, FEAT = cfg
    CH, HI, SUB, HALF = F // NZ, F // 2, F // NZ // 2, NZ // 2
    batch = lax.axis_index("batch")
    row, col = lax.axis_index("row"), lax.axis_index("col")
    z, yh, k = batch // (YH * NC), (batch // NC) % YH, batch % NC
    other = 1 - k

    def zz(d):
        return (z + d + NZ) % NZ

    def at_z(d):
        return {"batch": zz(d) * (YH * NC) + yh * NC + k}

    sibling = {"batch": batch - k + other}
    partner = {"batch": z * (YH * NC) + (1 - yh) * NC + k}
    xs = [{"col": (col + d) % NX} for d in range(1, NX)]
    ys = [{"row": (row + d) % NY} for d in range(1, NY)]

    copies = []

    def send(src, dst, dev):
        n = len(copies)
        c = pltpu.make_async_remote_copy(src_ref=src, dst_ref=dst, send_sem=send_sem.at[n],
                                         recv_sem=recv_sem.at[n], device_id=dev, device_id_type=MESH)
        copies.append(c)
        c.start()
        return c

    def lanes(p, w):
        return pl.ds(pl.multiple_of(p * w, 128), w)

    def rows(p, w):
        return pl.ds(pl.multiple_of(p * w, w), w)

    barrier = pltpu.get_barrier_semaphore()
    peers = [sibling, partner] + [at_z(d) for d in range(1, NZ)] + xs + ys
    for dev in peers:
        pl.semaphore_signal(barrier, inc=1, device_id=dev, device_id_type=MESH)
    pl.semaphore_wait(barrier, len(peers))

    get_b = send(b_ref, bx, sibling)
    get_a = send(a_ref.at[:, lanes(other, HI)], ax, sibling)

    def slab(n, acc):
        av = a_ref[rows(n, 16), :].astype(F32)
        bv = b_ref[rows(n, 16), :].astype(F32)
        new = (av, av * av, bv, bv * bv, av * bv)
        return tuple(o + v[:8] + v[8:] for o, v in zip(acc, new))

    sums = lax.fori_loop(0, S // 16, slab, tuple(jnp.zeros((8, F), F32) for _ in range(5)))
    for n, v in enumerate(sums):
        st_loc[n:n + 1, :] = jnp.sum(v, axis=0, keepdims=True)
    st_loc[5:8, :] = jnp.zeros((3, F), F32)
    st1 = send(st_loc, st_sib, sibling)

    get_b.wait_recv()
    get_a.wait_recv()

    def gram(d):
        at = lanes(zz(d), CH)
        tn = (((0,), (0,)), ((), ()))
        h[d % NZ] = lax.dot_general(b_ref[:, at], a_ref[:, lanes(k, HI)], tn, preferred_element_type=F32) + \
            lax.dot_general(bx[:, at], ax[...], tn, preferred_element_type=F32)

    R, L = 0, 1
    SGN = (1, -1)

    def part(d, s):
        return h[d % NZ, s * SUB:(s + 1) * SUB, :]

    arrive = {}
    gram(HALF)
    for di, s in ((R, 0), (L, 1)):
        rx0[di] = part(HALF, s).astype(BF16)
        arrive[0, di, s] = send(rx0.at[di], rx.at[0, di, s], at_z(SGN[di]))
    st1.wait_recv()
    st_chip[...] = st_loc[...] + st_sib[...]
    st2 = [send(st_chip.at[:, lanes(zz(d), CH)], st_rs.at[z], at_z(d)) for d in range(1, NZ)]
    st_rs[z] = st_chip[:, lanes(z, CH)]
    st3 = st4 = None
    for t in range(1, HALF):
        d = HALF - t
        gram(d)
        gram(-d)
        for di, s in ((R, 1), (L, 0), (R, 0), (L, 1)):
            if (t - 1, di, s) in arrive:
                arrive[t - 1, di, s].wait_recv()
                rx[t - 1, di, s] = (rx[t - 1, di, s].astype(F32) + part(SGN[di] * d, s)).astype(BF16)
            else:
                rx[t - 1, di, s] = part(SGN[di] * d, s).astype(BF16)
            arrive[t, di, s] = send(rx.at[t - 1, di, s], rx.at[t, di, s], at_z(SGN[di]))
        if t == 1:
            for c in st2:
                c.wait_recv()
            v = st_rs[0]
            for n in range(1, NZ):
                v = v + st_rs[n]
            st_zs[...] = v
            st3 = send(st_zs, st_yin, partner)
        if t == min(2, HALF - 1):
            st3.wait_recv()
            st[:, lanes(z, CH)] = st_zs[...] + st_yin[...]
            st4 = [send(st.at[:, lanes(z, CH)], st.at[:, lanes(z, CH)], at_z(d)) for d in range(1, NZ)]
    gram(0)
    swap = {}
    for s in (1, 0):
        t = HALF - 1
        arrive[t, R, s].wait_recv()
        arrive[t, L, s].wait_recv()
        hy[s] = (part(0, s) + rx[t, R, s].astype(F32) + rx[t, L, s].astype(F32)).astype(BF16)
        swap[s] = send(hy.at[s], hyin.at[s], partner)

    for c in st4:
        c.wait_recv()
    ma = st[0:1, :] * (1.0 / N)
    va = st[1:2, :] * (1.0 / N) - ma * ma + EPSILON
    mb = st[2:3, :] * (1.0 / N)
    vb = st[3:4, :] * (1.0 / N) - mb * mb + EPSILON
    ia, ib = lax.rsqrt(va), lax.rsqrt(vb)
    cd = (st[4:5, :] * (1.0 / N) - mb * ma) * (ia * ib)
    for n, v in enumerate((ma, va, ia, mb, vb, ib, cd)):
        vec[n:n + 1, :] = v
    own_diag = row == col
    diag_f = own_diag.astype(F32)
    lane = lax.broadcasted_iota(jnp.int32, (CH, CH), 1)
    eye = lax.broadcasted_iota(jnp.int32, (CH, CH), 0) == lane

    def to_col(v):
        return jnp.sum(jnp.where(eye, v, 0.0), axis=1, keepdims=True)

    def to_row(v):
        return jnp.sum(jnp.where(eye, v, 0.0), axis=0, keepdims=True)

    def diag_mask(zc, half, height, offset):
        jj = col * F + zc * CH + offset + lax.broadcasted_iota(jnp.int32, (height, HI), 0)
        ii = row * F + half * HI + lax.broadcasted_iota(jnp.int32, (height, HI), 1)
        return jj == ii

    mine = lanes(z, CH)
    mbc, ibc = to_col(vec[3:4, mine]), to_col(vec[5:6, mine])
    mar, iar, cdr = vec[0:1, lanes(k, HI)], vec[2:3, lanes(k, HI)], vec[6:7, lanes(k, HI)]
    got = {}
    for s in (1, 0):
        swap[s].wait_recv()
        tot = hy[s].astype(F32) + hyin[s].astype(F32)
        sl = slice(s * SUB, (s + 1) * SUB)
        outer = ibc[sl] * iar
        corr = (tot * (1.0 / N) - mbc[sl] * mar) * outer
        on = diag_mask(z, k, SUB, s * SUB)
        slope = jnp.where(on, -2.0 * (1.0 - cdr), 2.0 * LAMBDA_OFF * corr)
        at = (k, pl.ds(pl.multiple_of(z * CH + s * SUB, SUB), SUB))
        sh[at] = (slope * outer).astype(BF16)
        for di in (R, L):
            got[1, di, s] = send(sh.at[at], sh.at[at], at_z(SGN[di]))
        got[0, s] = send(sh.at[at], sh.at[at], sibling)

    rtv[...] = jnp.zeros_like(rtv)
    sav[...] = jnp.zeros_like(sav)

    def chunk(m):
        zc = zz(m)
        at = lanes(zc, CH)
        mbr, vbr, ibr, cdc = vec[3:4, at], vec[4:5, at], vec[5:6, at], vec[6:7, at]
        mbc, vbc = to_col(mbr), to_col(vbr)
        ct = jnp.zeros((CH, 1), F32)
        shift = jnp.zeros((CH, 1), F32)
        back = jnp.zeros((S, CH), F32)
        for half in range(2):
            w = slice(half * HI, (half + 1) * HI)
            sb = sh[half, rows(zc, CH), :]
            sf = sb.astype(F32)
            q = jnp.where(diag_mask(zc, half, CH, 0), 0.0, sf * sf)
            ct = ct + jnp.sum(q * vec[1:2, w], axis=1, keepdims=True)
            shift = shift + jnp.sum(sf * vec[0:1, w], axis=1, keepdims=True)
            rtv[0:1, w] += jnp.sum(q * vbc, axis=0, keepdims=True)
            sav[0:1, w] += jnp.sum(sf * mbc, axis=0, keepdims=True)
            back = back + lax.dot_general(a_ref[:, w], sb, (((1,), (1,)), ((), ())), preferred_element_type=F32)
        ct = to_row(ct) * vbr * (0.5 / LAMBDA_OFF)
        ls[pl.ds(zc, 1), :] = ct
        ct = ct + diag_f * (-2.0 * (1.0 - cdc) * cdc)
        grad = back - to_row(shift) - (ibr * ibr * ct) * (b_ref[:, at].astype(F32) - mbr)
        gb[m % NZ] = grad.astype(BF16)

    PB, PA = S // NY, S // NX
    order = [0] + [x for t in range(1, HALF) for x in (t, NZ - t)] + [HALF]
    groups = [[0]] + [[t, NZ - t] for t in range(1, HALF)] + [[HALF]]

    def scatter_b(ms):
        out = []
        for m in ms:
            for d in range(1, NY):
                q = (row + d) % NY
                out.append(send(gb.at[m, rows(q, PB), :], gbrs.at[m, row], ys[d - 1]))
        return out

    def gather_b(ms, arrived):
        for c in arrived:
            c.wait_recv()
        out = []
        for m in ms:
            v = gb[m, rows(row, PB), :].astype(F32)
            for d in range(1, NY):
                v = v + gbrs[m, (row + d) % NY].astype(F32)
            gbt[m, rows(row, PB), :] = v.astype(BF16)
            for d in range(1, NY):
                at = (m, rows(row, PB))
                out.append(send(gbt.at[at], gbt.at[at], ys[d - 1]))
        return out

    sib = {(0, s): got[0, s] for s in (0, 1)}
    scat, gath = [], []

    def group_compute(g):
        for m in groups[g]:
            for s in (1, 0):
                sib[m, s].wait_recv()
            chunk(m)
        scat.append(scatter_b(groups[g]))

    for t in range(1, HALF + 1):
        for di, s in ((R, 1), (L, 0), (R, 0), (L, 1)):
            if (t, di, s) not in got:
                continue
            got[t, di, s].wait_recv()
            m = (-SGN[di] * t) % NZ
            at = (k, pl.ds(pl.multiple_of(zz(m) * CH + s * SUB, SUB), SUB))
            if t < HALF - 1 or (t == HALF - 1 and s == (0 if di == R else 1)):
                got[t + 1, di, s] = send(sh.at[at], sh.at[at], at_z(SGN[di]))
            sib[m, s] = send(sh.at[at], sh.at[at], sibling)
        group_compute(t - 1)
        if t >= 2:
            gath.append(gather_b(groups[t - 2], scat[t - 2]))
    group_compute(HALF)
    gath.append(gather_b(groups[HALF - 1], scat[HALF - 1]))

    scat_a = []
    for half in range(2):
        w = slice(half * HI, (half + 1) * HI)
        mar, var, iar, cdr = vec[0:1, w], vec[1:2, w], vec[2:3, w], vec[6:7, w]
        acc = jnp.dot(b_ref[...], sh[half], preferred_element_type=F32)
        rt = rtv[0:1, w] * var * (0.5 / LAMBDA_OFF) + diag_f * (-2.0 * (1.0 - cdr) * cdr)
        grad = acc - sav[0:1, w] - (iar * iar * rt) * (a_ref[:, w].astype(F32) - mar)
        ga[half] = grad.astype(BF16)
        scat_a.append([send(ga.at[half, rows((col + d) % NX, PA), :], gars.at[half, col], xs[d - 1])
                       for d in range(1, NX)])

    cdv = vec[6:7, :]
    part_loss = 0.5 * jnp.sum(jnp.sum(ls[...], axis=0, keepdims=True), axis=1, keepdims=True) + \
        diag_f * jnp.sum(jnp.square(1.0 - cdv), axis=1, keepdims=True)
    lx[col] = jnp.broadcast_to(part_loss, (8, 128))
    loss_x = [send(lx.at[col], lx.at[col], dev) for dev in xs]

    gath.append(gather_b(groups[HALF], scat[HALF]))

    gath_a = []
    for half in range(2):
        for c in scat_a[half]:
            c.wait_recv()
        v = ga[half, rows(col, PA), :].astype(F32)
        for d in range(1, NX):
            v = v + gars[half, (col + d) % NX].astype(F32)
        at = (half, rows(col, PA))
        gat[at] = v.astype(BF16)
        gath_a.append([send(gat.at[at], gat.at[at], dev) for dev in xs])

    for c in loss_x:
        c.wait_recv()
    v = lx[0]
    for n in range(1, NX):
        v = v + lx[n]
    ly[row] = v
    loss_y = [send(ly.at[row], ly.at[row], dev) for dev in ys]

    for g, ms in enumerate(groups):
        for c in gath[g]:
            c.wait_recv()
        for m in ms:
            ob_ref[:, lanes(zz(m), CH)] = gbt[m].astype(F32)
    for c in loss_y:
        c.wait_recv()
    v = ly[0]
    for n in range(1, NY):
        v = v + ly[n]
    loss_ref[0, 0] = v[0, 0] / FEAT
    for half in range(2):
        for c in gath_a[half]:
            c.wait_recv()
        oa_ref[:, half * HI:(half + 1) * HI] = gat[half].astype(F32)
    for c in copies:
        c.wait_send()
    assert len(copies) <= NDMA


def build(mesh, NZ, YH, samples, feat):
    NX, NY = mesh.shape["col"], mesh.shape["row"]

    def on_device(a, b):
        S, F = a.shape
        CH, HI, SUB, HALF = F // NZ, F // 2, F // NZ // 2, NZ // 2
        cfg = (NZ, YH, NX, NY, S, F, samples, feat)
        vmem = pl.BlockSpec(memory_space=pltpu.VMEM)
        V = pltpu.VMEM
        ga, gb, loss = pl.pallas_call(
            functools.partial(kernel, cfg),
            out_shape=(jax.ShapeDtypeStruct((S, F), F32), jax.ShapeDtypeStruct((S, F), F32),
                       jax.ShapeDtypeStruct((1, 1), F32)),
            in_specs=[vmem, vmem],
            out_specs=(vmem, vmem, pl.BlockSpec(memory_space=pltpu.SMEM)),
            scratch_shapes=[
                V((S, HI), BF16), V((S, F), BF16),
                V((8, F), F32), V((8, F), F32), V((8, F), F32), V((NZ, 8, CH), F32), V((8, CH), F32),
                V((8, CH), F32), V((8, F), F32), V((8, F), F32),
                V((NZ, CH, HI), F32), V((HALF, 2, 2, SUB, HI), BF16), V((2, SUB, HI), BF16),
                V((2, SUB, HI), BF16), V((2, SUB, HI), BF16),
                V((2, F, HI), BF16),
                V((NZ, S, CH), BF16), V((NZ, NY, S // NY, CH), BF16), V((NZ, S, CH), BF16),
                V((2, S, HI), BF16), V((2, NX, S // NX, HI), BF16), V((2, S, HI), BF16),
                V((8, F), F32), V((8, F), F32), V((NZ, CH), F32), V((NX, 8, 128), F32), V((NY, 8, 128), F32),
                pltpu.SemaphoreType.DMA((NDMA,)), pltpu.SemaphoreType.DMA((NDMA,)),
            ],
            compiler_params=pltpu.CompilerParams(collective_id=0, has_side_effects=True,
                                                 vmem_limit_bytes=48 * 1024 * 1024),
            name="twins",
        )(a, b)
        return ga, gb, loss.reshape(())

    placed = (P("batch", "row"), P("batch", "col"))
    return jax.shard_map(on_device, mesh=mesh, in_specs=placed, out_specs=placed + (P(),), check_vma=False)


def solution(mesh):
    return build(mesh, 8, 2, 8192, 4096)
```

```python
import functools

import jax
import jax.numpy as jnp
from jax import lax
from jax.experimental import pallas as pl
from jax.experimental.pallas import tpu as pltpu
from jax.sharding import PartitionSpec as P

EPSILON = 1e-05
LAMBDA_OFF = 0.0051
MESH = pl.DeviceIdType.MESH
F32, BF16 = jnp.float32, jnp.bfloat16
NC = 2
NDMA = 160
NLOC = 32


def kernel(cfg, a_hbm, b_hbm, oa_ref, ob_ref, loss_ref,
           a_ref, b_ref, ax, bx, st_loc, st_sib, st_chip, st_rs, st_zs, st_yin, st, vec,
           h, rx, rx0, hy, hyin, sh, gb, gbe, gbs, gbm, gbt, ga, gars, gat, rtv, sav, ls, lx, ly,
           send_sem, recv_sem, loc_sem):
    NZ, YH, NX, NY, S, F, N, FEAT = cfg
    CH, HI, SUB, HALF = F // NZ, F // 2, F // NZ // 2, NZ // 2
    batch = lax.axis_index("batch")
    row, col = lax.axis_index("row"), lax.axis_index("col")
    z, yh, k = batch // (YH * NC), (batch // NC) % YH, batch % NC
    other = 1 - k

    def zz(d):
        return (z + d + NZ) % NZ

    def at_z(d):
        return {"batch": zz(d) * (YH * NC) + yh * NC + k}

    sibling = {"batch": batch - k + other}
    partner = {"batch": z * (YH * NC) + (1 - yh) * NC + k}
    xs = [{"col": (col + d) % NX} for d in range(1, NX)]
    ys = [{"row": (row + d) % NY} for d in range(1, NY)]

    buddy = {"row": row + 1 - 2 * (row % 2)}
    other_mid = {"row": NY - 1 - row}
    is_mid = (row == 1) | (row == 2)
    is_end = (row == 0) | (row == 3)

    copies = []

    def make(src, dst, dev, role=None):
        n = len(copies)
        c = pltpu.make_async_remote_copy(src_ref=src, dst_ref=dst, send_sem=send_sem.at[n],
                                         recv_sem=recv_sem.at[n], device_id=dev, device_id_type=MESH)
        copies.append((c, role))
        return c

    def send(src, dst, dev):
        c = make(src, dst, dev)
        c.start()
        return c

    local = []

    def keep(src, dst, role=None):
        c = pltpu.make_async_copy(src, dst, loc_sem.at[len(local)])
        local.append((c, role))
        return c

    def lanes(p, w):
        return pl.ds(pl.multiple_of(p * w, 128), w)

    def rows(p, w):
        return pl.ds(pl.multiple_of(p * w, w), w)

    load = [keep(a_hbm, a_ref), keep(b_hbm, b_ref)]
    for c in load:
        c.start()

    barrier = pltpu.get_barrier_semaphore()
    peers = [sibling, partner] + [at_z(d) for d in range(1, NZ)] + xs + ys
    for dev in peers:
        pl.semaphore_signal(barrier, inc=1, device_id=dev, device_id_type=MESH)
    pl.semaphore_wait(barrier, len(peers))

    get_b = send(b_hbm, bx, sibling)
    get_a = send(a_hbm.at[:, lanes(other, HI)], ax, sibling)
    for c in load:
        c.wait()

    def slab(n, acc):
        av = a_ref[rows(n, 16), :].astype(F32)
        bv = b_ref[rows(n, 16), :].astype(F32)
        new = (av, av * av, bv, bv * bv, av * bv)
        return tuple(o + v[:8] + v[8:] for o, v in zip(acc, new))

    sums = lax.fori_loop(0, S // 16, slab, tuple(jnp.zeros((8, F), F32) for _ in range(5)))
    for n, v in enumerate(sums):
        st_loc[n:n + 1, :] = jnp.sum(v, axis=0, keepdims=True)
    st_loc[5:8, :] = jnp.zeros((3, F), F32)
    st1 = send(st_loc, st_sib, sibling)

    get_b.wait_recv()
    get_a.wait_recv()

    def gram(d):
        at = lanes(zz(d), CH)
        tn = (((0,), (0,)), ((), ()))
        h[d % NZ] = lax.dot_general(b_ref[:, at], a_ref[:, lanes(k, HI)], tn, preferred_element_type=F32) + \
            lax.dot_general(bx[:, at], ax[...], tn, preferred_element_type=F32)

    R, L = 0, 1
    SGN = (1, -1)

    def part(d, s):
        return h[d % NZ, s * SUB:(s + 1) * SUB, :]

    arrive = {}
    gram(HALF)
    for di, s in ((R, 0), (L, 1)):
        rx0[di] = part(HALF, s).astype(BF16)
        arrive[0, di, s] = send(rx0.at[di], rx.at[0, di, s], at_z(SGN[di]))
    for t in range(1, HALF):
        d = HALF - t
        gram(d)
        gram(-d)
        for di, s in ((R, 1), (L, 0), (R, 0), (L, 1)):
            if t == 1 and (di, s) == (R, 0):
                st1.wait_recv()
                st_chip[...] = st_loc[...] + st_sib[...]
                st2 = [send(st_chip.at[:, lanes(zz(e), CH)], st_rs.at[z], at_z(e)) for e in range(1, NZ)]
                st_rs[z] = st_chip[:, lanes(z, CH)]
            if (t - 1, di, s) in arrive:
                arrive[t - 1, di, s].wait_recv()
                rx[t - 1, di, s] = (rx[t - 1, di, s].astype(F32) + part(SGN[di] * d, s)).astype(BF16)
            else:
                rx[t - 1, di, s] = part(SGN[di] * d, s).astype(BF16)
            arrive[t, di, s] = send(rx.at[t - 1, di, s], rx.at[t, di, s], at_z(SGN[di]))
        if t == min(2, HALF - 1):
            for c in st2:
                c.wait_recv()
            v = st_rs[0]
            for n in range(1, NZ):
                v = v + st_rs[n]
            st_zs[...] = v
            st3 = send(st_zs, st_yin, partner)
    gram(0)
    swap = {}
    for s in (1, 0):
        t = HALF - 1
        arrive[t, R, s].wait_recv()
        arrive[t, L, s].wait_recv()
        hy[s] = (part(0, s) + rx[t, R, s].astype(F32) + rx[t, L, s].astype(F32)).astype(BF16)
        swap[s] = send(hy.at[s], hyin.at[s], partner)

    st3.wait_recv()
    st[:, lanes(z, CH)] = st_zs[...] + st_yin[...]
    st4 = [send(st.at[:, lanes(z, CH)], st.at[:, lanes(z, CH)], at_z(d)) for d in range(1, NZ)]

    for c in st4:
        c.wait_recv()
    ma = st[0:1, :] * (1.0 / N)
    va = st[1:2, :] * (1.0 / N) - ma * ma + EPSILON
    mb = st[2:3, :] * (1.0 / N)
    vb = st[3:4, :] * (1.0 / N) - mb * mb + EPSILON
    ia, ib = lax.rsqrt(va), lax.rsqrt(vb)
    cd = (st[4:5, :] * (1.0 / N) - mb * ma) * (ia * ib)
    for n, v in enumerate((ma, va, ia, mb, vb, ib, cd)):
        vec[n:n + 1, :] = v
    own_diag = row == col
    diag_f = own_diag.astype(F32)
    lane = lax.broadcasted_iota(jnp.int32, (CH, CH), 1)
    eye = lax.broadcasted_iota(jnp.int32, (CH, CH), 0) == lane

    def to_col(v):
        return jnp.sum(jnp.where(eye, v, 0.0), axis=1, keepdims=True)

    def to_row(v):
        return jnp.sum(jnp.where(eye, v, 0.0), axis=0, keepdims=True)

    def diag_mask(zc, half, height, offset):
        jj = col * F + zc * CH + offset + lax.broadcasted_iota(jnp.int32, (height, HI), 0)
        ii = row * F + half * HI + lax.broadcasted_iota(jnp.int32, (height, HI), 1)
        return jj == ii

    mine = lanes(z, CH)
    mbc, ibc = to_col(vec[3:4, mine]), to_col(vec[5:6, mine])
    mar, iar, cdr = vec[0:1, lanes(k, HI)], vec[2:3, lanes(k, HI)], vec[6:7, lanes(k, HI)]
    got = {}
    for s in (1, 0):
        swap[s].wait_recv()
        tot = hy[s].astype(F32) + hyin[s].astype(F32)
        sl = slice(s * SUB, (s + 1) * SUB)
        outer = ibc[sl] * iar
        corr = (tot * (1.0 / N) - mbc[sl] * mar) * outer
        on = diag_mask(z, k, SUB, s * SUB)
        slope = jnp.where(on, -2.0 * (1.0 - cdr), 2.0 * LAMBDA_OFF * corr)
        at = (k, pl.ds(pl.multiple_of(z * CH + s * SUB, SUB), SUB))
        sh[at] = (slope * outer).astype(BF16)
        for di in (R, L):
            got[1, di, s] = send(sh.at[at], sh.at[at], at_z(SGN[di]))
        got[0, s] = send(sh.at[at], sh.at[at], sibling)

    rtv[...] = jnp.zeros_like(rtv)
    sav[...] = jnp.zeros_like(sav)

    def chunk(m, slot):
        zc = zz(m)
        at = lanes(zc, CH)
        mbr, vbr, ibr, cdc = vec[3:4, at], vec[4:5, at], vec[5:6, at], vec[6:7, at]
        mbc, vbc = to_col(mbr), to_col(vbr)
        ct = jnp.zeros((CH, 1), F32)
        shift = jnp.zeros((CH, 1), F32)
        back = jnp.zeros((S, CH), F32)
        for half in range(2):
            w = slice(half * HI, (half + 1) * HI)
            sb = sh[half, rows(zc, CH), :]
            sf = sb.astype(F32)
            q = jnp.where(diag_mask(zc, half, CH, 0), 0.0, sf * sf)
            ct = ct + jnp.sum(q * vec[1:2, w], axis=1, keepdims=True)
            shift = shift + jnp.sum(sf * vec[0:1, w], axis=1, keepdims=True)
            rtv[0:1, w] += jnp.sum(q * vbc, axis=0, keepdims=True)
            sav[0:1, w] += jnp.sum(sf * mbc, axis=0, keepdims=True)
            back = back + lax.dot_general(a_ref[:, w], sb, (((1,), (1,)), ((), ())), preferred_element_type=F32)
        ct = to_row(ct) * vbr * (0.5 / LAMBDA_OFF)
        ls[pl.ds(zc, 1), :] = ct
        ct = ct + diag_f * (-2.0 * (1.0 - cdc) * cdc)
        grad = back - to_row(shift) - (ibr * ibr * ct) * (b_ref[:, at].astype(F32) - mbr)
        gb[slot] = grad.astype(BF16)

    PA, SH = S // NX, S // 2
    own_half, far_half = pl.ds(pl.multiple_of((row // 2) * SH, SH), SH), pl.ds(pl.multiple_of((1 - row // 2) * SH, SH), SH)
    order = [0] + [x for t in range(1, HALF) for x in (t, NZ - t)] + [HALF]
    groups = [[0]] + [[2 * t - 1, 2 * t] for t in range(1, HALF)] + [[NZ - 1]]
    out_at = [lanes(zz(m), CH) for m in order]
    pair, cross, both, outs, give = {}, {}, {}, {}, {}
    for g, ps in enumerate(groups):
        sl = pl.ds(ps[0], len(ps))
        pair[g] = make(gb.at[sl], gbe.at[sl], buddy, "end")
        cross[g] = make(gbs.at[sl, far_half], gbm.at[sl], other_mid, "mid")
        both[g] = make(gbt.at[sl, own_half], gbt.at[sl, own_half], other_mid, "mid")
        give[g] = [make(gbt.at[p, own_half], ob_ref.at[own_half, out_at[p]], buddy, "mid") for p in ps]
        give[g] += [make(gbt.at[p, far_half], ob_ref.at[far_half, out_at[p]], buddy, "mid") for p in ps]
        outs[g] = [keep(gbt.at[p], ob_ref.at[:, out_at[p]], "mid") for p in ps]

    def step1(g):
        @pl.when(is_end)
        def _():
            pair[g].start()

    def step2(g):
        @pl.when(is_mid)
        def _():
            pair[g].wait_recv()
            for p in groups[g]:
                gbs[p] = (gb[p].astype(F32) + gbe[p].astype(F32)).astype(BF16)
            cross[g].start()

    def step3(g):
        @pl.when(is_mid)
        def _():
            cross[g].wait_recv()
            for p in groups[g]:
                gbt[p, own_half, :] = (gbs[p, own_half, :].astype(F32) + gbm[p].astype(F32)).astype(BF16)
            both[g].start()
            for c in give[g][:len(groups[g])]:
                c.start()

    def step4(g):
        @pl.when(is_mid)
        def _():
            both[g].wait_recv()
            for c in give[g][len(groups[g]):]:
                c.start()
            for c in outs[g]:
                c.start()

    STEPS = (step1, step2, step3, step4)

    def advance(n):
        for lag in (1, 2, 3):
            if 0 <= n - lag < len(groups):
                STEPS[lag](n - lag)

    sib = {(0, s): got[0, s] for s in (0, 1)}

    def group_compute(g):
        for p in groups[g]:
            for s in (1, 0):
                sib[order[p], s].wait_recv()
            chunk(order[p], p)
        step1(g)

    for t in range(1, HALF + 1):
        for di, s in ((R, 1), (L, 1), (R, 0), (L, 0)):
            if (t, di, s) not in got:
                continue
            got[t, di, s].wait_recv()
            m = (-SGN[di] * t) % NZ
            at = (k, pl.ds(pl.multiple_of(zz(m) * CH + s * SUB, SUB), SUB))
            if t < HALF - 1 or (t == HALF - 1 and s == (0 if di == R else 1)):
                got[t + 1, di, s] = send(sh.at[at], sh.at[at], at_z(SGN[di]))
            sib[m, s] = send(sh.at[at], sh.at[at], sibling)
        group_compute(t - 1)
        advance(t - 1)
    group_compute(HALF)

    scat_a = []
    for half in range(2):
        w = slice(half * HI, (half + 1) * HI)
        mar, var, iar, cdr = vec[0:1, w], vec[1:2, w], vec[2:3, w], vec[6:7, w]
        acc = jnp.dot(b_ref[...], sh[half], preferred_element_type=F32)
        rt = rtv[0:1, w] * var * (0.5 / LAMBDA_OFF) + diag_f * (-2.0 * (1.0 - cdr) * cdr)
        grad = acc - sav[0:1, w] - (iar * iar * rt) * (a_ref[:, w].astype(F32) - mar)
        ga[half] = grad.astype(BF16)
        scat_a.append([send(ga.at[half, rows((col + d) % NX, PA), :], gars.at[half, col], xs[d - 1])
                       for d in range(1, NX)])

    cdv = vec[6:7, :]
    part_loss = 0.5 * jnp.sum(jnp.sum(ls[...], axis=0, keepdims=True), axis=1, keepdims=True) + \
        diag_f * jnp.sum(jnp.square(1.0 - cdv), axis=1, keepdims=True)
    lx[col] = jnp.broadcast_to(part_loss, (8, 128))
    loss_x = [send(lx.at[col], lx.at[col], dev) for dev in xs]

    advance(HALF)
    advance(HALF + 1)

    gath_a = []
    for half in range(2):
        for c in scat_a[half]:
            c.wait_recv()
        v = ga[half, rows(col, PA), :].astype(F32)
        for d in range(1, NX):
            v = v + gars[half, (col + d) % NX].astype(F32)
        gat[half] = v.astype(BF16)
        at = (rows(col, PA), pl.ds(half * HI, HI))
        gath_a.append([send(gat.at[half], oa_ref.at[at], dev) for dev in xs])
        keep(gat.at[half], oa_ref.at[at]).start()
        advance(HALF + 2 + half)

    for c in loss_x:
        c.wait_recv()
    v = lx[0]
    for n in range(1, NX):
        v = v + lx[n]
    ly[row] = v
    loss_y = [send(ly.at[row], ly.at[row], dev) for dev in ys]

    for c in loss_y:
        c.wait_recv()
    v = ly[0]
    for n in range(1, NY):
        v = v + ly[n]
    loss_ref[0, 0] = v[0, 0] / FEAT
    for half in range(2):
        for c in gath_a[half]:
            c.wait_recv()

    @pl.when(is_end)
    def _():
        for g in range(len(groups)):
            for c in give[g]:
                c.wait_recv()

    for role, cond in (("mid", is_mid), ("end", is_end)):
        @pl.when(cond)
        def _():
            for c, r in copies:
                if r == role:
                    c.wait_send()
            for c, r in local:
                if r == role:
                    c.wait()

    for c, r in copies:
        if r is None:
            c.wait_send()
    for c, r in local[2:]:
        if r is None:
            c.wait()
    assert len(copies) <= NDMA and len(local) <= NLOC


def build(mesh, NZ, YH, samples, feat):
    NX, NY = mesh.shape["col"], mesh.shape["row"]

    def on_device(a, b):
        S, F = a.shape
        CH, HI, SUB, HALF = F // NZ, F // 2, F // NZ // 2, NZ // 2
        cfg = (NZ, YH, NX, NY, S, F, samples, feat)
        hbm = pl.BlockSpec(memory_space=pl.ANY)
        V = pltpu.VMEM
        ga, gb, loss = pl.pallas_call(
            functools.partial(kernel, cfg),
            out_shape=(jax.ShapeDtypeStruct((S, F), BF16), jax.ShapeDtypeStruct((S, F), BF16),
                       jax.ShapeDtypeStruct((1, 1), F32)),
            in_specs=[pl.BlockSpec(memory_space=pltpu.HBM)] * 2,
            out_specs=(hbm, hbm, pl.BlockSpec(memory_space=pltpu.SMEM)),
            scratch_shapes=[
                V((S, F), BF16), V((S, F), BF16), V((S, HI), BF16), V((S, F), BF16),
                V((8, F), F32), V((8, F), F32), V((8, F), F32), V((NZ, 8, CH), F32), V((8, CH), F32),
                V((8, CH), F32), V((8, F), F32), V((8, F), F32),
                V((NZ, CH, HI), F32), V((HALF, 2, 2, SUB, HI), BF16), V((2, SUB, HI), BF16),
                V((2, SUB, HI), BF16), V((2, SUB, HI), BF16),
                V((2, F, HI), BF16),
                V((NZ, S, CH), BF16), V((NZ, S, CH), BF16), V((NZ, S, CH), BF16), V((NZ, S // 2, CH), BF16),
                V((NZ, S, CH), BF16),
                V((2, S, HI), BF16), V((2, NX, S // NX, HI), BF16), V((2, S // NX, HI), BF16),
                V((8, F), F32), V((8, F), F32), V((NZ, CH), F32), V((NX, 8, 128), F32), V((NY, 8, 128), F32),
                pltpu.SemaphoreType.DMA((NDMA,)), pltpu.SemaphoreType.DMA((NDMA,)), pltpu.SemaphoreType.DMA((NLOC,)),
            ],
            compiler_params=pltpu.CompilerParams(collective_id=0, has_side_effects=True,
                                                 vmem_limit_bytes=62 * 1024 * 1024),
            name="twins",
        )(a, b)
        return ga.astype(F32), gb.astype(F32), loss.reshape(())

    placed = (P("batch", "row"), P("batch", "col"))
    return jax.shard_map(on_device, mesh=mesh, in_specs=placed, out_specs=placed + (P(),), check_vma=False)


def solution(mesh):
    return build(mesh, 8, 2, 8192, 4096)
```

```python
import functools

import jax
import jax.numpy as jnp
from jax import lax
from jax.experimental import pallas as pl
from jax.experimental.pallas import tpu as pltpu
from jax.sharding import PartitionSpec as P

EPSILON = 1e-05
LAMBDA_OFF = 0.0051
MESH = pl.DeviceIdType.MESH
F32, BF16 = jnp.float32, jnp.bfloat16
NC = 2
NLOC = 18
NS = 4


def kernel(cfg, a_hbm, b_hbm, oa_ref, ob_ref, loss_ref,
           a_ref, b_ref, ax, bx, st_loc, st_sib, st_chip, st_rs, st_zs, st_yin, st, vec,
           h, rx, rx0, hy, hyin, sh, gb, gbe, gbs, gbm, gbt, ga, gars, gat, rtv, sav, ls, lx, ly,
           send_sem, recv_sem, rs_sem, ag_sem, sib_sem, y_sem, loc_sem):
    NZ, YH, NX, NY, S, F, N, FEAT = cfg
    CH, HI, W, HALF = F // NZ, F // 2, F // 2 // NS, NZ // 2
    batch = lax.axis_index("batch")
    row, col = lax.axis_index("row"), lax.axis_index("col")
    z, yh, k = batch // (YH * NC), (batch // NC) % YH, batch % NC
    other = 1 - k

    def zz(d):
        return (z + d + NZ) % NZ

    def at_z(d):
        return {"batch": zz(d) * (YH * NC) + yh * NC + k}

    sibling = {"batch": batch - k + other}
    partner = {"batch": z * (YH * NC) + (1 - yh) * NC + k}
    xs = [{"col": (col + d) % NX} for d in range(1, NX)]
    ys = [{"row": (row + d) % NY} for d in range(1, NY)]
    buddy = {"row": row + 1 - 2 * (row % 2)}
    other_mid = {"row": NY - 1 - row}
    is_mid = (row == 1) | (row == 2)
    is_end = (row == 0) | (row == 3)

    names = ("b", "a", "st1", "st2", "st3", "st4", "rs", "swap", "ag", "sib", "pair", "cross", "both", "give",
             "scat", "gath", "lx", "ly")

    def make(name, src, dst, dev, sem=None):
        n = names.index(name)
        return pltpu.make_async_remote_copy(src_ref=src, dst_ref=dst, send_sem=send_sem.at[n],
                                            recv_sem=recv_sem.at[n] if sem is None else sem,
                                            device_id=dev, device_id_type=MESH)

    def send(name, src, dst, dev, sem=None):
        c = make(name, src, dst, dev, sem)
        c.start()
        return c

    def got_all(name, ref, sem=None):
        make(name, ref, ref, sibling, sem).wait_recv()

    def sent_all(name, ref):
        make(name, ref, ref, sibling).wait_send()

    local = []

    def keep(src, dst, role=None):
        c = pltpu.make_async_copy(src, dst, loc_sem.at[len(local)])
        local.append((c, role))
        return c

    def lanes(p, w):
        return pl.ds(pl.multiple_of(p * w, 128), w)

    def rows(p, w):
        return pl.ds(pl.multiple_of(p * w, w), w)

    load = [keep(a_hbm, a_ref), keep(b_hbm, b_ref)]
    for c in load:
        c.start()

    barrier = pltpu.get_barrier_semaphore()
    peers = [sibling, partner] + [at_z(d) for d in range(1, NZ)] + xs + ys
    for dev in peers:
        pl.semaphore_signal(barrier, inc=1, device_id=dev, device_id_type=MESH)
    pl.semaphore_wait(barrier, len(peers))

    get_b = send("b", b_hbm, bx, sibling)
    get_a = send("a", a_hbm.at[:, lanes(other, HI)], ax, sibling)
    for c in load:
        c.wait()

    def slab(n, acc):
        av = a_ref[rows(n, 16), :].astype(F32)
        bv = b_ref[rows(n, 16), :].astype(F32)
        new = (av, av * av, bv, bv * bv, av * bv)
        return tuple(o + v[:8] + v[8:] for o, v in zip(acc, new))

    sums = lax.fori_loop(0, S // 16, slab, tuple(jnp.zeros((8, F), F32) for _ in range(5)))
    for n, v in enumerate(sums):
        st_loc[n:n + 1, :] = jnp.sum(v, axis=0, keepdims=True)
    st_loc[5:8, :] = jnp.zeros((3, F), F32)
    st1 = send("st1", st_loc, st_sib, sibling)

    get_b.wait_recv()
    get_a.wait_recv()

    def gram(d):
        at = lanes(zz(d), CH)
        tn = (((0,), (0,)), ((), ()))
        h[d % NZ] = lax.dot_general(b_ref[:, at], a_ref[:, lanes(k, HI)], tn, preferred_element_type=F32) + \
            lax.dot_general(bx[:, at], ax[...], tn, preferred_element_type=F32)

    R, L = 0, 1
    SGN = (1, -1)

    def part(d, s):
        return h[d % NZ, :, s * W:(s + 1) * W]

    arrive = {}
    gram(HALF)
    for s in range(NS):
        di = s % 2
        rx0[s] = part(HALF, s).astype(BF16)
        arrive[0, di, s] = send("rs", rx0.at[s], rx.at[0, di, s], at_z(SGN[di]), rs_sem.at[0, di, s])
    st1.wait_recv()
    st_chip[...] = st_loc[...] + st_sib[...]
    for e in range(1, NZ):
        send("st2", st_chip.at[:, lanes(zz(e), CH)], st_rs.at[z], at_z(e))
    st_rs[z] = st_chip[:, lanes(z, CH)]
    early = [((s + 1) % 2, s) for s in (1, 0, 3, 2)]
    late = [(s % 2, s) for s in range(NS)]
    for t in range(1, HALF):
        d = HALF - t
        gram(d)
        gram(-d)
        for di, s in early + late if t == 1 else early[:2] + late[:2] + early[2:] + late[2:]:
            if (t - 1, di, s) in arrive:
                arrive[t - 1, di, s].wait_recv()
                rx[t - 1, di, s] = (rx[t - 1, di, s].astype(F32) + part(SGN[di] * d, s)).astype(BF16)
            else:
                rx[t - 1, di, s] = part(SGN[di] * d, s).astype(BF16)
            arrive[t, di, s] = send("rs", rx.at[t - 1, di, s], rx.at[t, di, s], at_z(SGN[di]), rs_sem.at[t, di, s])
        if t == min(2, HALF - 1):
            got_all("st2", st_rs.at[pl.ds(0, NZ - 1)])
            v = st_rs[0]
            for n in range(1, NZ):
                v = v + st_rs[n]
            st_zs[...] = v
            st3 = send("st3", st_zs, st_yin, partner)
    gram(0)
    swap = {}
    for s in range(NS):
        t = HALF - 1
        arrive[t, R, s].wait_recv()
        arrive[t, L, s].wait_recv()
        hy[s] = (part(0, s) + rx[t, R, s].astype(F32) + rx[t, L, s].astype(F32)).astype(BF16)
        swap[s] = send("swap", hy.at[s], hyin.at[s], partner, y_sem.at[s])
    st3.wait_recv()
    st[:, lanes(z, CH)] = st_zs[...] + st_yin[...]
    for d in range(1, NZ):
        send("st4", st.at[:, lanes(z, CH)], st.at[:, lanes(z, CH)], at_z(d))
    got_all("st4", st_rs.at[pl.ds(0, NZ - 1)])

    ma = st[0:1, :] * (1.0 / N)
    va = st[1:2, :] * (1.0 / N) - ma * ma + EPSILON
    mb = st[2:3, :] * (1.0 / N)
    vb = st[3:4, :] * (1.0 / N) - mb * mb + EPSILON
    ia, ib = lax.rsqrt(va), lax.rsqrt(vb)
    cd = (st[4:5, :] * (1.0 / N) - mb * ma) * (ia * ib)
    for n, v in enumerate((ma, va, ia, mb, vb, ib, cd)):
        vec[n:n + 1, :] = v
    own_diag = row == col
    diag_f = own_diag.astype(F32)
    lane = lax.broadcasted_iota(jnp.int32, (CH, CH), 1)
    eye = lax.broadcasted_iota(jnp.int32, (CH, CH), 0) == lane

    def to_col(v):
        return jnp.sum(jnp.where(eye, v, 0.0), axis=1, keepdims=True)

    def to_row(v):
        return jnp.sum(jnp.where(eye, v, 0.0), axis=0, keepdims=True)

    def diag_mask(zc, half, piece):
        jj = col * F + zc * CH + lax.broadcasted_iota(jnp.int32, (CH, W), 0)
        ii = row * F + half * HI + piece * W + lax.broadcasted_iota(jnp.int32, (CH, W), 1)
        return jj == ii

    mine = lanes(z, CH)
    mbc, ibc = to_col(vec[3:4, mine]), to_col(vec[5:6, mine])
    groups = [[0]] + [[2 * t - 1, 2 * t] for t in range(1, HALF)] + [[NZ - 1]]
    order = [0] + [x for t in range(1, HALF) for x in (t, NZ - t)] + [HALF]
    sib_of = {order[p]: g for g, ps in enumerate(groups) for p in ps}
    got = {}

    def to_sibling(m, s):
        at = (k, s, rows(zz(m), CH))
        n = sib_of[m % NZ] + (s if m % NZ == HALF else 0)
        send("sib", sh.at[at], sh.at[at], sibling, sib_sem.at[n])

    for s in range(NS):
        swap[s].wait_recv()
        tot = hy[s].astype(F32) + hyin[s].astype(F32)
        at_i = pl.ds(pl.multiple_of(k * HI + s * W, 128), W)
        mar, iar, cdr = vec[0:1, at_i], vec[2:3, at_i], vec[6:7, at_i]
        outer = ibc * iar
        corr = (tot * (1.0 / N) - mbc * mar) * outer
        slope = jnp.where(diag_mask(z, k, s), -2.0 * (1.0 - cdr), 2.0 * LAMBDA_OFF * corr)
        at = (k, s, rows(z, CH))
        sh[at] = (slope * outer).astype(BF16)
        for di in (R, L):
            got[1, di, s] = send("ag", sh.at[at], sh.at[at], at_z(SGN[di]), ag_sem.at[0, di, s])
        to_sibling(0, s)

    rtv[...] = jnp.zeros_like(rtv)
    sav[...] = jnp.zeros_like(sav)

    def piece(m, s):
        zc = zz(m)
        at = lanes(zc, CH)
        mbc, vbc = to_col(vec[3:4, at]), to_col(vec[4:5, at])
        ct = jnp.zeros((CH, W), F32)
        shift = jnp.zeros((CH, W), F32)
        for half in range(2):
            w = slice(half * HI + s * W, half * HI + (s + 1) * W)
            sf = sh[half, s, rows(zc, CH), :].astype(F32)
            q = jnp.where(diag_mask(zc, half, s), 0.0, sf * sf)
            ct = ct + q * vec[1:2, w]
            shift = shift + sf * vec[0:1, w]
            rtv[0:1, w] += jnp.sum(q * vbc, axis=0, keepdims=True)
            sav[0:1, w] += jnp.sum(sf * mbc, axis=0, keepdims=True)
        return ct, shift

    def chunk(m, slot, terms):
        zc = zz(m)
        at = lanes(zc, CH)
        mbr, vbr, ibr, cdc = vec[3:4, at], vec[4:5, at], vec[5:6, at], vec[6:7, at]
        ct, shift = terms[0]
        for c, v in terms[1:]:
            ct, shift = ct + c, shift + v
        ct = to_row(jnp.sum(ct, axis=1, keepdims=True)) * vbr * (0.5 / LAMBDA_OFF)
        shift = to_row(jnp.sum(shift, axis=1, keepdims=True))
        back = jnp.zeros((S, CH), F32)
        for half in range(2):
            sb = jnp.concatenate([sh[half, s, rows(zc, CH), :] for s in range(NS)], axis=1)
            back = back + lax.dot_general(a_ref[:, half * HI:(half + 1) * HI], sb, (((1,), (1,)), ((), ())),
                                          preferred_element_type=F32)
        ls[pl.ds(zc, 1), :] = ct
        ct = ct + diag_f * (-2.0 * (1.0 - cdc) * cdc)
        grad = back - shift - (ibr * ibr * ct) * (b_ref[:, at].astype(F32) - mbr)
        gb[slot] = grad.astype(BF16)

    PA, SH = S // NX, S // 2
    own_half, far_half = rows(row // 2, SH), rows(1 - row // 2, SH)
    out_at = [lanes(zz(m), CH) for m in order]
    pair, cross, both, outs, give = [], [], [], [], []
    for p in range(NZ):
        n = NS + 3 * p
        pair.append(make("pair", gb.at[p], gbe.at[p], buddy, y_sem.at[n]))
        cross.append(make("cross", gbs.at[p, far_half], gbm.at[p], other_mid, y_sem.at[n + 1]))
        both.append(make("both", gbt.at[p, own_half], gbt.at[p, own_half], other_mid, y_sem.at[n + 2]))
        give.append([make("give", gbt.at[p, w], ob_ref.at[w, out_at[p]], buddy) for w in (own_half, far_half)])
        outs.append(keep(gbt.at[p], ob_ref.at[:, out_at[p]], "mid"))

    def step1(p):
        @pl.when(is_end)
        def _():
            pair[p].start()

    def step2(*ps):
        @pl.when(is_mid)
        def _():
            for p in ps:
                pair[p].wait_recv()
                gbs[p] = (gb[p].astype(F32) + gbe[p].astype(F32)).astype(BF16)
                cross[p].start()

    def step3(*ps):
        @pl.when(is_mid)
        def _():
            for p in ps:
                cross[p].wait_recv()
                gbt[p, own_half, :] = (gbs[p, own_half, :].astype(F32) + gbm[p].astype(F32)).astype(BF16)
                both[p].start()
                give[p][0].start()

    def step4(*ps):
        @pl.when(is_mid)
        def _():
            for p in ps:
                both[p].wait_recv()
                give[p][1].start()
                outs[p].start()

    def group_compute(g):
        got_all("sib", sh.at[0, :, pl.ds(0, len(groups[g]) * CH)], sib_sem.at[g])
        for p in groups[g]:
            chunk(order[p], p, [piece(order[p], s) for s in range(NS)])
            step1(p)

    def advance(g):
        for n, step in ((g - 1, step2), (g - 2, step3), (g - 3, step4)):
            if 0 <= n < len(groups):
                step(*groups[n])

    for t in range(1, HALF):
        for s in range(NS):
            for di in (R, L):
                got[t, di, s].wait_recv()
                m = (-SGN[di] * t) % NZ
                at = (k, s, rows(zz(m), CH))
                if t < HALF - 1 or s % 2 == di:
                    got[t + 1, di, s] = send("ag", sh.at[at], sh.at[at], at_z(SGN[di]), ag_sem.at[t, di, s])
                to_sibling(m, s)
        group_compute(t - 1)
        advance(t - 1)
    group_compute(HALF - 1)

    advance(HALF - 1)

    terms = []
    scat_sem = NS + 3 * NZ

    def last(s):
        got_all("sib", sh.at[0, s, pl.ds(0, CH)], sib_sem.at[HALF + s])
        terms.append(piece(HALF, s))

    def send_a(s):
        for half in range(2):
            w = slice(half * HI + s * W, half * HI + (s + 1) * W)
            mar, var, iar, cdr = vec[0:1, w], vec[1:2, w], vec[2:3, w], vec[6:7, w]
            acc = jnp.dot(b_ref[...], sh[half, s], preferred_element_type=F32)
            rt = rtv[0:1, w] * var * (0.5 / LAMBDA_OFF) + diag_f * (-2.0 * (1.0 - cdr) * cdr)
            grad = acc - sav[0:1, w] - (iar * iar * rt) * (a_ref[:, w].astype(F32) - mar)
            ga[s, :, half * W:(half + 1) * W] = grad.astype(BF16)
        for d in range(1, NX):
            send("scat", ga.at[s, rows((col + d) % NX, PA), :], gars.at[s, col], xs[d - 1], y_sem.at[scat_sem + s])

    def finish_a(s):
        got_all("scat", gars.at[s, pl.ds(0, NX - 1)], y_sem.at[scat_sem + s])
        v = ga[s, rows(col, PA), :].astype(F32)
        for d in range(1, NX):
            v = v + gars[s, (col + d) % NX].astype(F32)
        gat[s] = v.astype(BF16)
        for half in range(2):
            src = gat.at[s, :, pl.ds(half * W, W)]
            at = (rows(col, PA), pl.ds(half * HI + s * W, W))
            for dev in xs:
                send("gath", src, oa_ref.at[at], dev)
            keep(src, oa_ref.at[at]).start()

    for s in range(NS):
        got[HALF, s % 2, s].wait_recv()
        to_sibling(HALF, s)
        if s:
            last(s - 1)
            if s < NS - 1:
                send_a(s - 1)
    last(NS - 1)
    chunk(HALF, NZ - 1, terms)
    step1(NZ - 1)

    cdv = vec[6:7, :]
    part_loss = 0.5 * jnp.sum(jnp.sum(ls[...], axis=0, keepdims=True), axis=1, keepdims=True) + \
        diag_f * jnp.sum(jnp.square(1.0 - cdv), axis=1, keepdims=True)
    lx[col] = jnp.broadcast_to(part_loss, (8, 128))
    for dev in xs:
        send("lx", lx.at[col], lx.at[col], dev)
    step2(*groups[HALF - 1])
    for s in range(NS - 2, NS):
        send_a(s)
    step3(*groups[HALF - 2])
    step4(*groups[HALF - 3])
    step2(NZ - 1)
    step3(*groups[HALF - 1])
    finish_a(0)
    step4(*groups[HALF - 2])
    got_all("lx", lx.at[pl.ds(0, NX - 1)])
    v = lx[0]
    for n in range(1, NX):
        v = v + lx[n]
    ly[row] = v
    for dev in ys:
        send("ly", ly.at[row], ly.at[row], dev)
    step3(NZ - 1)
    finish_a(1)
    step4(*groups[HALF - 1])
    finish_a(2)
    step4(NZ - 1)
    finish_a(3)

    got_all("ly", ly.at[pl.ds(0, NY - 1)])
    v = ly[0]
    for n in range(1, NY):
        v = v + ly[n]
    loss_ref[0, 0] = v[0, 0] / FEAT

    for c in (get_b, get_a, st1, st3):
        c.wait_send()
    for name, ref in (("st2", st_rs.at[pl.ds(0, NZ - 1)]), ("st4", st_rs.at[pl.ds(0, NZ - 1)]),
                      ("rs", sh.at[0, :, pl.ds(0, (NZ - 1) * CH)]), ("swap", hy),
                      ("ag", sh.at[0, :, pl.ds(0, (NZ - 1) * CH)]), ("sib", sh.at[0]),
                      ("scat", gars.at[:, pl.ds(0, NX - 1)]), ("gath", gars.at[:, pl.ds(0, NX - 1)]),
                      ("lx", lx.at[pl.ds(0, NX - 1)]), ("ly", ly.at[pl.ds(0, NY - 1)])):
        sent_all(name, ref)

    @pl.when(is_end)
    def _():
        got_all("give", gbt)
        sent_all("pair", gb)

    @pl.when(is_mid)
    def _():
        sent_all("cross", gbm)
        sent_all("both", gbm)
        sent_all("give", gbt)
        for c, r in local:
            if r == "mid":
                c.wait()

    got_all("gath", gars.at[:, pl.ds(0, NX - 1)])
    for c, r in local[2:]:
        if r is None:
            c.wait()
    assert len(local) <= NLOC


def build(mesh, NZ, YH, samples, feat):
    NX, NY = mesh.shape["col"], mesh.shape["row"]

    def on_device(a, b):
        S, F = a.shape
        CH, HI, W, HALF = F // NZ, F // 2, F // 2 // NS, NZ // 2
        cfg = (NZ, YH, NX, NY, S, F, samples, feat)
        hbm = pl.BlockSpec(memory_space=pl.ANY)
        V = pltpu.VMEM
        ga, gb, loss = pl.pallas_call(
            functools.partial(kernel, cfg),
            out_shape=(jax.ShapeDtypeStruct((S, F), BF16), jax.ShapeDtypeStruct((S, F), BF16),
                       jax.ShapeDtypeStruct((1, 1), F32)),
            in_specs=[pl.BlockSpec(memory_space=pltpu.HBM)] * 2,
            out_specs=(hbm, hbm, pl.BlockSpec(memory_space=pltpu.SMEM)),
            scratch_shapes=[
                V((S, F), BF16), V((S, F), BF16), V((S, HI), BF16), V((S, F), BF16),
                V((8, F), F32), V((8, F), F32), V((8, F), F32), V((NZ, 8, CH), F32), V((8, CH), F32),
                V((8, CH), F32), V((8, F), F32), V((8, F), F32),
                V((NZ, CH, HI), F32), V((HALF, 2, NS, CH, W), BF16), V((NS, CH, W), BF16),
                V((NS, CH, W), BF16), V((NS, CH, W), BF16), V((2, NS, F, W), BF16),
                V((NZ, S, CH), BF16), V((NZ, S, CH), BF16), V((NZ, S, CH), BF16), V((NZ, S // 2, CH), BF16),
                V((NZ, S, CH), BF16),
                V((NS, S, 2 * W), BF16), V((NS, NX, S // NX, 2 * W), BF16), V((NS, S // NX, 2 * W), BF16),
                V((8, F), F32), V((8, F), F32), V((NZ, CH), F32), V((NX, 8, 128), F32), V((NY, 8, 128), F32),
                pltpu.SemaphoreType.DMA((18,)), pltpu.SemaphoreType.DMA((18,)),
                pltpu.SemaphoreType.DMA((HALF, 2, NS)), pltpu.SemaphoreType.DMA((HALF, 2, NS)),
                pltpu.SemaphoreType.DMA((HALF + NS,)), pltpu.SemaphoreType.DMA((2 * NS + 3 * NZ,)),
                pltpu.SemaphoreType.DMA((NLOC,)),
            ],
            compiler_params=pltpu.CompilerParams(collective_id=0, has_side_effects=True,
                                                 vmem_limit_bytes=53 * 1024 * 1024),
            name="twins",
        )(a, b)
        return ga.astype(F32), gb.astype(F32), loss.reshape(())

    placed = (P("batch", "row"), P("batch", "col"))
    return jax.shard_map(on_device, mesh=mesh, in_specs=placed, out_specs=placed + (P(),), check_vma=False)


def solution(mesh):
    return build(mesh, 8, 2, 8192, 4096)
```

```python
import functools

import jax
import jax.numpy as jnp
from jax import lax
from jax.experimental import pallas as pl
from jax.experimental.pallas import tpu as pltpu
from jax.sharding import PartitionSpec as P

EPSILON = 1e-05
LAMBDA_OFF = 0.0051
MESH = pl.DeviceIdType.MESH
F32, BF16 = jnp.float32, jnp.bfloat16
NC = 2
NLOC = 18
NS = 4


def kernel(cfg, a_hbm, b_hbm, oa_ref, ob_ref, loss_ref,
           a_ref, b_ref, ax, bx, st_loc, st_sib, st_chip, st_rs, st_zs, st_yin, st, vec,
           h, rx, rx0, hy, hyin, sh, gb, gbe, gbs, gbm, gbt, ga, gars, gat, rtv, sav, ls, lx, ly,
           send_sem, recv_sem, rs_sem, ag_sem, sib_sem, y_sem, loc_sem):
    NZ, YH, NX, NY, S, F, N, FEAT = cfg
    CH, HI, W, HALF = F // NZ, F // 2, F // 2 // NS, NZ // 2
    batch = lax.axis_index("batch")
    row, col = lax.axis_index("row"), lax.axis_index("col")
    z, yh, k = batch // (YH * NC), (batch // NC) % YH, batch % NC
    other = 1 - k

    def zz(d):
        return (z + d + NZ) % NZ

    def at_z(d):
        return {"batch": zz(d) * (YH * NC) + yh * NC + k}

    sibling = {"batch": batch - k + other}
    partner = {"batch": z * (YH * NC) + (1 - yh) * NC + k}
    xs = [{"col": (col + d) % NX} for d in range(1, NX)]
    ys = [{"row": (row + d) % NY} for d in range(1, NY)]
    buddy = {"row": row + 1 - 2 * (row % 2)}
    other_mid = {"row": NY - 1 - row}
    is_mid = (row == 1) | (row == 2)
    is_end = (row == 0) | (row == 3)

    names = ("b0", "b", "a", "st1", "st2", "st3", "st4", "rs", "swap", "ag", "sib", "pair", "cross", "both", "give",
             "scat", "gath", "lx", "ly")

    def make(name, src, dst, dev, sem=None):
        n = names.index(name)
        return pltpu.make_async_remote_copy(src_ref=src, dst_ref=dst, send_sem=send_sem.at[n],
                                            recv_sem=recv_sem.at[n] if sem is None else sem,
                                            device_id=dev, device_id_type=MESH)

    def send(name, src, dst, dev, sem=None):
        c = make(name, src, dst, dev, sem)
        c.start()
        return c

    def got_all(name, ref, sem=None):
        make(name, ref, ref, sibling, sem).wait_recv()

    def sent_all(name, ref):
        make(name, ref, ref, sibling).wait_send()

    local = []

    def keep(src, dst, role=None):
        c = pltpu.make_async_copy(src, dst, loc_sem.at[len(local)])
        local.append((c, role))
        return c

    def lanes(p, w):
        return pl.ds(pl.multiple_of(p * w, 128), w)

    def rows(p, w):
        return pl.ds(pl.multiple_of(p * w, w), w)

    load = [keep(a_hbm, a_ref), keep(b_hbm, b_ref)]
    for c in load:
        c.start()

    barrier = pltpu.get_barrier_semaphore()
    peers = [sibling, partner] + [at_z(d) for d in range(1, NZ)] + xs + ys
    for dev in peers:
        pl.semaphore_signal(barrier, inc=1, device_id=dev, device_id_type=MESH)
    pl.semaphore_wait(barrier, len(peers))

    get_a = send("a", a_hbm.at[:, lanes(other, HI)], ax, sibling)
    get_b = None
    for d in range(HALF, HALF - NZ, -1):
        at = lanes(zz(d), CH)
        c = send("b0" if d == HALF else "b", b_hbm.at[:, at], bx.at[:, at], sibling)
        get_b = get_b or c
    for c in load:
        c.wait()

    def slab(n, acc):
        av = a_ref[rows(n, 16), :].astype(F32)
        bv = b_ref[rows(n, 16), :].astype(F32)
        new = (av, av * av, bv, bv * bv, av * bv)
        return tuple(o + v[:8] + v[8:] for o, v in zip(acc, new))

    sums = lax.fori_loop(0, S // 16, slab, tuple(jnp.zeros((8, F), F32) for _ in range(5)))
    for n, v in enumerate(sums):
        st_loc[n:n + 1, :] = jnp.sum(v, axis=0, keepdims=True)
    st_loc[5:8, :] = jnp.zeros((3, F), F32)
    st1 = send("st1", st_loc, st_sib, sibling)

    get_b.wait_recv()
    get_a.wait_recv()

    def gram(d):
        at = lanes(zz(d), CH)
        tn = (((0,), (0,)), ((), ()))
        h[d % NZ] = lax.dot_general(b_ref[:, at], a_ref[:, lanes(k, HI)], tn, preferred_element_type=F32) + \
            lax.dot_general(bx[:, at], ax[...], tn, preferred_element_type=F32)

    R, L = 0, 1
    SGN = (1, -1)

    def part(d, s):
        return h[d % NZ, :, s * W:(s + 1) * W]

    arrive = {}
    gram(HALF)
    for s in range(NS):
        di = s % 2
        rx0[s] = part(HALF, s).astype(BF16)
        arrive[0, di, s] = send("rs", rx0.at[s], rx.at[0, di, s], at_z(SGN[di]), rs_sem.at[0, di, s])
    got_all("b", bx.at[:, pl.ds(0, F - CH)])
    st1.wait_recv()
    st_chip[...] = st_loc[...] + st_sib[...]
    for e in range(1, NZ):
        send("st2", st_chip.at[:, lanes(zz(e), CH)], st_rs.at[z], at_z(e))
    st_rs[z] = st_chip[:, lanes(z, CH)]
    early = [((s + 1) % 2, s) for s in (1, 0, 3, 2)]
    late = [(s % 2, s) for s in range(NS)]
    for t in range(1, HALF):
        d = HALF - t
        gram(d)
        gram(-d)
        for di, s in early + late if t == 1 else early[:2] + late[:2] + early[2:] + late[2:]:
            if (t - 1, di, s) in arrive:
                arrive[t - 1, di, s].wait_recv()
                rx[t - 1, di, s] = (rx[t - 1, di, s].astype(F32) + part(SGN[di] * d, s)).astype(BF16)
            else:
                rx[t - 1, di, s] = part(SGN[di] * d, s).astype(BF16)
            arrive[t, di, s] = send("rs", rx.at[t - 1, di, s], rx.at[t, di, s], at_z(SGN[di]), rs_sem.at[t, di, s])
        if t == min(2, HALF - 1):
            got_all("st2", st_rs.at[pl.ds(0, NZ - 1)])
            v = st_rs[0]
            for n in range(1, NZ):
                v = v + st_rs[n]
            st_zs[...] = v
            st3 = send("st3", st_zs, st_yin, partner)
    gram(0)
    swap = {}
    for s in range(NS):
        t = HALF - 1
        arrive[t, R, s].wait_recv()
        arrive[t, L, s].wait_recv()
        hy[s] = (part(0, s) + rx[t, R, s].astype(F32) + rx[t, L, s].astype(F32)).astype(BF16)
        swap[s] = send("swap", hy.at[s], hyin.at[s], partner, y_sem.at[s])
    st3.wait_recv()
    st[:, lanes(z, CH)] = st_zs[...] + st_yin[...]
    for d in range(1, NZ):
        send("st4", st.at[:, lanes(z, CH)], st.at[:, lanes(z, CH)], at_z(d))
    got_all("st4", st_rs.at[pl.ds(0, NZ - 1)])

    ma = st[0:1, :] * (1.0 / N)
    va = st[1:2, :] * (1.0 / N) - ma * ma + EPSILON
    mb = st[2:3, :] * (1.0 / N)
    vb = st[3:4, :] * (1.0 / N) - mb * mb + EPSILON
    ia, ib = lax.rsqrt(va), lax.rsqrt(vb)
    cd = (st[4:5, :] * (1.0 / N) - mb * ma) * (ia * ib)
    for n, v in enumerate((ma, va, ia, mb, vb, ib, cd)):
        vec[n:n + 1, :] = v
    own_diag = row == col
    diag_f = own_diag.astype(F32)
    lane = lax.broadcasted_iota(jnp.int32, (CH, CH), 1)
    eye = lax.broadcasted_iota(jnp.int32, (CH, CH), 0) == lane

    def to_col(v):
        return jnp.sum(jnp.where(eye, v, 0.0), axis=1, keepdims=True)

    def to_row(v):
        return jnp.sum(jnp.where(eye, v, 0.0), axis=0, keepdims=True)

    def diag_mask(zc, half, piece):
        jj = col * F + zc * CH + lax.broadcasted_iota(jnp.int32, (CH, W), 0)
        ii = row * F + half * HI + piece * W + lax.broadcasted_iota(jnp.int32, (CH, W), 1)
        return jj == ii

    mine = lanes(z, CH)
    mbc, ibc = to_col(vec[3:4, mine]), to_col(vec[5:6, mine])
    groups = [[0]] + [[2 * t - 1, 2 * t] for t in range(1, HALF)] + [[NZ - 1]]
    order = [0] + [x for t in range(1, HALF) for x in (t, NZ - t)] + [HALF]
    sib_of = {order[p]: g for g, ps in enumerate(groups) for p in ps}
    got = {}

    def to_sibling(m, s):
        at = (k, s, rows(zz(m), CH))
        n = sib_of[m % NZ] + (s if m % NZ == HALF else 0)
        send("sib", sh.at[at], sh.at[at], sibling, sib_sem.at[n])

    for s in range(NS):
        swap[s].wait_recv()
        tot = hy[s].astype(F32) + hyin[s].astype(F32)
        at_i = pl.ds(pl.multiple_of(k * HI + s * W, 128), W)
        mar, iar, cdr = vec[0:1, at_i], vec[2:3, at_i], vec[6:7, at_i]
        outer = ibc * iar
        corr = (tot * (1.0 / N) - mbc * mar) * outer
        slope = jnp.where(diag_mask(z, k, s), -2.0 * (1.0 - cdr), 2.0 * LAMBDA_OFF * corr)
        at = (k, s, rows(z, CH))
        sh[at] = (slope * outer).astype(BF16)
        for di in (R, L):
            got[1, di, s] = send("ag", sh.at[at], sh.at[at], at_z(SGN[di]), ag_sem.at[0, di, s])
        to_sibling(0, s)

    rtv[...] = jnp.zeros_like(rtv)
    sav[...] = jnp.zeros_like(sav)

    def piece(m, s):
        zc = zz(m)
        at = lanes(zc, CH)
        mbc, vbc = to_col(vec[3:4, at]), to_col(vec[4:5, at])
        ct = jnp.zeros((CH, W), F32)
        shift = jnp.zeros((CH, W), F32)
        for half in range(2):
            w = slice(half * HI + s * W, half * HI + (s + 1) * W)
            sf = sh[half, s, rows(zc, CH), :].astype(F32)
            q = jnp.where(diag_mask(zc, half, s), 0.0, sf * sf)
            ct = ct + q * vec[1:2, w]
            shift = shift + sf * vec[0:1, w]
            rtv[0:1, w] += jnp.sum(q * vbc, axis=0, keepdims=True)
            sav[0:1, w] += jnp.sum(sf * mbc, axis=0, keepdims=True)
        return ct, shift

    def chunk(m, slot, terms):
        zc = zz(m)
        at = lanes(zc, CH)
        mbr, vbr, ibr, cdc = vec[3:4, at], vec[4:5, at], vec[5:6, at], vec[6:7, at]
        ct, shift = terms[0]
        for c, v in terms[1:]:
            ct, shift = ct + c, shift + v
        ct = to_row(jnp.sum(ct, axis=1, keepdims=True)) * vbr * (0.5 / LAMBDA_OFF)
        shift = to_row(jnp.sum(shift, axis=1, keepdims=True))
        back = jnp.zeros((S, CH), F32)
        for half in range(2):
            sb = jnp.concatenate([sh[half, s, rows(zc, CH), :] for s in range(NS)], axis=1)
            back = back + lax.dot_general(a_ref[:, half * HI:(half + 1) * HI], sb, (((1,), (1,)), ((), ())),
                                          preferred_element_type=F32)
        ls[pl.ds(zc, 1), :] = ct
        ct = ct + diag_f * (-2.0 * (1.0 - cdc) * cdc)
        grad = back - shift - (ibr * ibr * ct) * (b_ref[:, at].astype(F32) - mbr)
        gb[slot] = grad.astype(BF16)

    PA, SH = S // NX, S // 2
    own_half, far_half = rows(row // 2, SH), rows(1 - row // 2, SH)
    out_at = [lanes(zz(m), CH) for m in order]
    other_end = {"row": (2 - row + NY) * (NY - 1) % NY}
    pair, cross, both, outs, give = [], [], [], [], []
    for p in range(NZ):
        n = NS + 4 * p
        pair.append([make("pair", gb.at[p, w], gbe.at[p, w], buddy, y_sem.at[n + 2 + i])
                     for i, w in enumerate((far_half, own_half))])
        cross.append(make("cross", gbs.at[p, far_half], gbm.at[p], other_mid, y_sem.at[n + 1]))
        both.append(make("both", gbt.at[p, own_half], gbt.at[p, own_half], other_mid, y_sem.at[n]))
        w = own_half if p >= NZ - 3 else far_half
        give.append([make("give", gbt.at[p, own_half], ob_ref.at[own_half, out_at[p]], buddy),
                     make("give", gbt.at[p, w], ob_ref.at[w, out_at[p]], other_end if p >= NZ - 3 else buddy)])
        outs.append(keep(gbt.at[p], ob_ref.at[:, out_at[p]], "mid"))

    def step1(p):
        @pl.when(is_end)
        def _():
            for c in pair[p]:
                c.start()

    def step2(*ps):
        @pl.when(is_mid)
        def _():
            for p in ps:
                pair[p][0].wait_recv()
                gbs[p, far_half, :] = (gb[p, far_half, :].astype(F32) + gbe[p, far_half, :].astype(F32)).astype(BF16)
                cross[p].start()

    def step3(*ps):
        @pl.when(is_mid)
        def _():
            for p in ps:
                pair[p][1].wait_recv()
                cross[p].wait_recv()
                v = gb[p, own_half, :].astype(F32) + gbe[p, own_half, :].astype(F32)
                gbt[p, own_half, :] = (v + gbm[p].astype(F32)).astype(BF16)
                both[p].start()
                give[p][0].start()
                if p >= NZ - 3:
                    give[p][1].start()

    def step4(*ps):
        @pl.when(is_mid)
        def _():
            for p in ps:
                both[p].wait_recv()
                if p < NZ - 3:
                    give[p][1].start()
                outs[p].start()

    def group_compute(g):
        got_all("sib", sh.at[0, :, pl.ds(0, len(groups[g]) * CH)], sib_sem.at[g])
        for p in groups[g]:
            chunk(order[p], p, [piece(order[p], s) for s in range(NS)])
            step1(p)

    def advance(g):
        for n, step in ((g - 1, step2), (g - 2, step3), (g - 3, step4)):
            if 0 <= n < len(groups):
                step(*groups[n])

    for t in range(1, HALF):
        for s in range(NS):
            for di in (R, L):
                got[t, di, s].wait_recv()
                m = (-SGN[di] * t) % NZ
                at = (k, s, rows(zz(m), CH))
                if t < HALF - 1 or s % 2 == di:
                    got[t + 1, di, s] = send("ag", sh.at[at], sh.at[at], at_z(SGN[di]), ag_sem.at[t, di, s])
                to_sibling(m, s)
        group_compute(t - 1)
        advance(t - 1)
    group_compute(HALF - 1)

    advance(HALF - 1)

    terms = []
    scat_sem = NS + 4 * NZ

    def last(s):
        got_all("sib", sh.at[0, s, pl.ds(0, CH)], sib_sem.at[HALF + s])
        terms.append(piece(HALF, s))

    def send_a(s):
        for half in range(2):
            w = slice(half * HI + s * W, half * HI + (s + 1) * W)
            mar, var, iar, cdr = vec[0:1, w], vec[1:2, w], vec[2:3, w], vec[6:7, w]
            acc = jnp.dot(b_ref[...], sh[half, s], preferred_element_type=F32)
            rt = rtv[0:1, w] * var * (0.5 / LAMBDA_OFF) + diag_f * (-2.0 * (1.0 - cdr) * cdr)
            grad = acc - sav[0:1, w] - (iar * iar * rt) * (a_ref[:, w].astype(F32) - mar)
            ga[s, :, half * W:(half + 1) * W] = grad.astype(BF16)
        for d in range(1, NX):
            send("scat", ga.at[s, rows((col + d) % NX, PA), :], gars.at[s, col], xs[d - 1], y_sem.at[scat_sem + s])

    def finish_a(s):
        got_all("scat", gars.at[s, pl.ds(0, NX - 1)], y_sem.at[scat_sem + s])
        v = ga[s, rows(col, PA), :].astype(F32)
        for d in range(1, NX):
            v = v + gars[s, (col + d) % NX].astype(F32)
        gat[s] = v.astype(BF16)
        for half in range(2):
            src = gat.at[s, :, pl.ds(half * W, W)]
            at = (rows(col, PA), pl.ds(half * HI + s * W, W))
            for dev in xs:
                send("gath", src, oa_ref.at[at], dev)
            keep(src, oa_ref.at[at]).start()

    for s in range(NS):
        got[HALF, s % 2, s].wait_recv()
        to_sibling(HALF, s)
        if s:
            last(s - 1)
            if s < NS - 1:
                send_a(s - 1)
    last(NS - 1)
    chunk(HALF, NZ - 1, terms)
    step1(NZ - 1)

    cdv = vec[6:7, :]
    part_loss = 0.5 * jnp.sum(jnp.sum(ls[...], axis=0, keepdims=True), axis=1, keepdims=True) + \
        diag_f * jnp.sum(jnp.square(1.0 - cdv), axis=1, keepdims=True)
    lx[col] = jnp.broadcast_to(part_loss, (8, 128))
    for dev in xs:
        send("lx", lx.at[col], lx.at[col], dev)
    step2(*groups[HALF - 1])
    for s in range(NS - 2, NS):
        send_a(s)
    step3(*groups[HALF - 2])
    step4(*groups[HALF - 3])
    step2(NZ - 1)
    step3(*groups[HALF - 1])
    finish_a(0)
    step4(*groups[HALF - 2])
    got_all("lx", lx.at[pl.ds(0, NX - 1)])
    v = lx[0]
    for n in range(1, NX):
        v = v + lx[n]
    ly[row] = v
    for dev in ys:
        send("ly", ly.at[row], ly.at[row], dev)
    finish_a(1)
    step3(NZ - 1)
    finish_a(2)
    step4(*groups[HALF - 1])
    finish_a(3)
    step4(NZ - 1)

    got_all("ly", ly.at[pl.ds(0, NY - 1)])
    v = ly[0]
    for n in range(1, NY):
        v = v + ly[n]
    loss_ref[0, 0] = v[0, 0] / FEAT

    for c in (get_b, get_a, st1, st3):
        c.wait_send()
    for name, ref in (("b", bx.at[:, pl.ds(0, F - CH)]), ("st2", st_rs.at[pl.ds(0, NZ - 1)]), ("st4", st_rs.at[pl.ds(0, NZ - 1)]),
                      ("rs", sh.at[0, :, pl.ds(0, (NZ - 1) * CH)]), ("swap", hy),
                      ("ag", sh.at[0, :, pl.ds(0, (NZ - 1) * CH)]), ("sib", sh.at[0]),
                      ("scat", gars.at[:, pl.ds(0, NX - 1)]), ("gath", gars.at[:, pl.ds(0, NX - 1)]),
                      ("lx", lx.at[pl.ds(0, NX - 1)]), ("ly", ly.at[pl.ds(0, NY - 1)])):
        sent_all(name, ref)

    @pl.when(is_end)
    def _():
        got_all("give", gbt)
        sent_all("pair", gb)

    @pl.when(is_mid)
    def _():
        sent_all("cross", gbm)
        sent_all("both", gbm)
        sent_all("give", gbt)
        for c, r in local:
            if r == "mid":
                c.wait()

    got_all("gath", gars.at[:, pl.ds(0, NX - 1)])
    for c, r in local[2:]:
        if r is None:
            c.wait()
    assert len(local) <= NLOC


def build(mesh, NZ, YH, samples, feat):
    NX, NY = mesh.shape["col"], mesh.shape["row"]

    def on_device(a, b):
        S, F = a.shape
        CH, HI, W, HALF = F // NZ, F // 2, F // 2 // NS, NZ // 2
        cfg = (NZ, YH, NX, NY, S, F, samples, feat)
        hbm = pl.BlockSpec(memory_space=pl.ANY)
        V = pltpu.VMEM
        ga, gb, loss = pl.pallas_call(
            functools.partial(kernel, cfg),
            out_shape=(jax.ShapeDtypeStruct((S, F), BF16), jax.ShapeDtypeStruct((S, F), BF16),
                       jax.ShapeDtypeStruct((1, 1), F32)),
            in_specs=[pl.BlockSpec(memory_space=pltpu.HBM)] * 2,
            out_specs=(hbm, hbm, pl.BlockSpec(memory_space=pltpu.SMEM)),
            scratch_shapes=[
                V((S, F), BF16), V((S, F), BF16), V((S, HI), BF16), V((S, F), BF16),
                V((8, F), F32), V((8, F), F32), V((8, F), F32), V((NZ, 8, CH), F32), V((8, CH), F32),
                V((8, CH), F32), V((8, F), F32), V((8, F), F32),
                V((NZ, CH, HI), F32), V((HALF, 2, NS, CH, W), BF16), V((NS, CH, W), BF16),
                V((NS, CH, W), BF16), V((NS, CH, W), BF16), V((2, NS, F, W), BF16),
                V((NZ, S, CH), BF16), V((NZ, S, CH), BF16), V((NZ, S, CH), BF16), V((NZ, S // 2, CH), BF16),
                V((NZ, S, CH), BF16),
                V((NS, S, 2 * W), BF16), V((NS, NX, S // NX, 2 * W), BF16), V((NS, S // NX, 2 * W), BF16),
                V((8, F), F32), V((8, F), F32), V((NZ, CH), F32), V((NX, 8, 128), F32), V((NY, 8, 128), F32),
                pltpu.SemaphoreType.DMA((19,)), pltpu.SemaphoreType.DMA((19,)),
                pltpu.SemaphoreType.DMA((HALF, 2, NS)), pltpu.SemaphoreType.DMA((HALF, 2, NS)),
                pltpu.SemaphoreType.DMA((HALF + NS,)), pltpu.SemaphoreType.DMA((2 * NS + 4 * NZ,)),
                pltpu.SemaphoreType.DMA((NLOC,)),
            ],
            compiler_params=pltpu.CompilerParams(collective_id=0, has_side_effects=True,
                                                 vmem_limit_bytes=53 * 1024 * 1024),
            name="twins",
        )(a, b)
        return ga.astype(F32), gb.astype(F32), loss.reshape(())

    placed = (P("batch", "row"), P("batch", "col"))
    return jax.shard_map(on_device, mesh=mesh, in_specs=placed, out_specs=placed + (P(),), check_vma=False)


def solution(mesh):
    return build(mesh, 8, 2, 8192, 4096)
```

```python
import functools

import jax
import jax.numpy as jnp
from jax import lax
from jax.experimental import pallas as pl
from jax.experimental.pallas import tpu as pltpu
from jax.sharding import PartitionSpec as P

EPSILON = 1e-05
LAMBDA_OFF = 0.0051
MESH = pl.DeviceIdType.MESH
F32, BF16 = jnp.float32, jnp.bfloat16
NC = 2
NLOC = 18
NS = 4


def kernel(cfg, a_hbm, b_hbm, oa_ref, ob_ref, loss_ref,
           a_ref, b_ref, ax, bx, st_loc, st_sib, st_chip, st_rs, st_zs, st_yin, st, vec,
           h, rx, rx0, hy, hyin, sh, gb, gbe, gbs, gbm, gbt, ga, gars, gat, rtv, sav, ls, lx, ly,
           send_sem, recv_sem, rs_sem, ag_sem, sib_sem, y_sem, loc_sem):
    NZ, YH, NX, NY, S, F, N, FEAT = cfg
    CH, HI, W, HALF = F // NZ, F // 2, F // 2 // NS, NZ // 2
    batch = lax.axis_index("batch")
    row, col = lax.axis_index("row"), lax.axis_index("col")
    z, yh, k = batch // (YH * NC), (batch // NC) % YH, batch % NC
    other = 1 - k

    def zz(d):
        return (z + d + NZ) % NZ

    def at_z(d):
        return {"batch": zz(d) * (YH * NC) + yh * NC + k}

    sibling = {"batch": batch - k + other}
    partner = {"batch": z * (YH * NC) + (1 - yh) * NC + k}
    xs = [{"col": (col + d) % NX} for d in range(1, NX)]
    ys = [{"row": (row + d) % NY} for d in range(1, NY)]
    buddy = {"row": row + 1 - 2 * (row % 2)}
    other_mid = {"row": NY - 1 - row}
    is_mid = (row == 1) | (row == 2)
    is_end = (row == 0) | (row == 3)

    names = ("b0", "b", "a", "st1", "st2", "st3", "st4", "rs", "swap", "ag", "sib", "pair", "cross", "both", "give",
             "scat", "gath", "lx", "ly")

    def make(name, src, dst, dev, sem=None):
        n = names.index(name)
        return pltpu.make_async_remote_copy(src_ref=src, dst_ref=dst, send_sem=send_sem.at[n],
                                            recv_sem=recv_sem.at[n] if sem is None else sem,
                                            device_id=dev, device_id_type=MESH)

    def send(name, src, dst, dev, sem=None):
        c = make(name, src, dst, dev, sem)
        c.start()
        return c

    def got_all(name, ref, sem=None):
        make(name, ref, ref, sibling, sem).wait_recv()

    def sent_all(name, ref):
        make(name, ref, ref, sibling).wait_send()

    local = []

    def keep(src, dst, role=None):
        c = pltpu.make_async_copy(src, dst, loc_sem.at[len(local)])
        local.append((c, role))
        return c

    def lanes(p, w):
        return pl.ds(pl.multiple_of(p * w, 128), w)

    def rows(p, w):
        return pl.ds(pl.multiple_of(p * w, w), w)

    load = [keep(a_hbm, a_ref), keep(b_hbm, b_ref)]
    for c in load:
        c.start()

    barrier = pltpu.get_barrier_semaphore()
    peers = [sibling, partner] + [at_z(d) for d in range(1, NZ)] + xs + ys
    for dev in peers:
        pl.semaphore_signal(barrier, inc=1, device_id=dev, device_id_type=MESH)
    pl.semaphore_wait(barrier, len(peers))

    get_a = send("a", a_hbm.at[:, lanes(other, HI)], ax, sibling)
    get_b = None
    for d in range(HALF, HALF - NZ, -1):
        at = lanes(zz(d), CH)
        c = send("b0" if d == HALF else "b", b_hbm.at[:, at], bx.at[:, at], sibling)
        get_b = get_b or c
    for c in load:
        c.wait()

    def slab(n, acc):
        av = a_ref[rows(n, 16), :].astype(F32)
        bv = b_ref[rows(n, 16), :].astype(F32)
        new = (av, av * av, bv, bv * bv, av * bv)
        return tuple(o + v[:8] + v[8:] for o, v in zip(acc, new))

    sums = lax.fori_loop(0, S // 16, slab, tuple(jnp.zeros((8, F), F32) for _ in range(5)))
    for n, v in enumerate(sums):
        st_loc[n:n + 1, :] = jnp.sum(v, axis=0, keepdims=True)
    st_loc[5:8, :] = jnp.zeros((3, F), F32)
    st1 = send("st1", st_loc, st_sib, sibling)

    get_b.wait_recv()
    get_a.wait_recv()

    def gram(d):
        at = lanes(zz(d), CH)
        tn = (((0,), (0,)), ((), ()))
        h[d % NZ] = lax.dot_general(b_ref[:, at], a_ref[:, lanes(k, HI)], tn, preferred_element_type=F32) + \
            lax.dot_general(bx[:, at], ax[...], tn, preferred_element_type=F32)

    R, L = 0, 1
    SGN = (1, -1)

    def part(d, s):
        return h[d % NZ, :, s * W:(s + 1) * W]

    arrive = {}
    gram(HALF)
    for s in range(NS):
        di = s % 2
        rx0[s] = part(HALF, s).astype(BF16)
        arrive[0, di, s] = send("rs", rx0.at[s], rx.at[0, di, s], at_z(SGN[di]), rs_sem.at[0, di, s])
    got_all("b", bx.at[:, pl.ds(0, F - CH)])
    st1.wait_recv()
    st_chip[...] = st_loc[...] + st_sib[...]
    for e in range(1, NZ):
        send("st2", st_chip.at[:, lanes(zz(e), CH)], st_rs.at[z], at_z(e))
    st_rs[z] = st_chip[:, lanes(z, CH)]
    early = [((s + 1) % 2, s) for s in (1, 0, 3, 2)]
    late = [(s % 2, s) for s in range(NS)]
    for t in range(1, HALF):
        d = HALF - t
        gram(d)
        gram(-d)
        for di, s in early + late if t == 1 else early[:2] + late[:2] + early[2:] + late[2:]:
            if (t - 1, di, s) in arrive:
                arrive[t - 1, di, s].wait_recv()
                rx[t - 1, di, s] = (rx[t - 1, di, s].astype(F32) + part(SGN[di] * d, s)).astype(BF16)
            else:
                rx[t - 1, di, s] = part(SGN[di] * d, s).astype(BF16)
            arrive[t, di, s] = send("rs", rx.at[t - 1, di, s], rx.at[t, di, s], at_z(SGN[di]), rs_sem.at[t, di, s])
        if t == min(2, HALF - 1):
            got_all("st2", st_rs.at[pl.ds(0, NZ - 1)])
            v = st_rs[0]
            for n in range(1, NZ):
                v = v + st_rs[n]
            st_zs[...] = v
            st3 = send("st3", st_zs, st_yin, partner)
    gram(0)
    swap = {}
    for s in range(NS):
        t = HALF - 1
        arrive[t, R, s].wait_recv()
        arrive[t, L, s].wait_recv()
        hy[s] = (part(0, s) + rx[t, R, s].astype(F32) + rx[t, L, s].astype(F32)).astype(BF16)
        swap[s] = send("swap", hy.at[s], hyin.at[s], partner, y_sem.at[s])
        if s == 1:
            st3.wait_recv()
            st[:, lanes(z, CH)] = st_zs[...] + st_yin[...]
            for d in range(1, NZ):
                send("st4", st.at[:, lanes(z, CH)], st.at[:, lanes(z, CH)], at_z(d))
    got_all("st4", st_rs.at[pl.ds(0, NZ - 1)])

    ma = st[0:1, :] * (1.0 / N)
    va = st[1:2, :] * (1.0 / N) - ma * ma + EPSILON
    mb = st[2:3, :] * (1.0 / N)
    vb = st[3:4, :] * (1.0 / N) - mb * mb + EPSILON
    ia, ib = lax.rsqrt(va), lax.rsqrt(vb)
    cd = (st[4:5, :] * (1.0 / N) - mb * ma) * (ia * ib)
    for n, v in enumerate((ma, va, ia, mb, vb, ib, cd)):
        vec[n:n + 1, :] = v
    own_diag = row == col
    diag_f = own_diag.astype(F32)
    lane = lax.broadcasted_iota(jnp.int32, (CH, CH), 1)
    eye = lax.broadcasted_iota(jnp.int32, (CH, CH), 0) == lane

    def to_col(v):
        return jnp.sum(jnp.where(eye, v, 0.0), axis=1, keepdims=True)

    def to_row(v):
        return jnp.sum(jnp.where(eye, v, 0.0), axis=0, keepdims=True)

    def diag_mask(zc, half, piece):
        jj = col * F + zc * CH + lax.broadcasted_iota(jnp.int32, (CH, W), 0)
        ii = row * F + half * HI + piece * W + lax.broadcasted_iota(jnp.int32, (CH, W), 1)
        return jj == ii

    mine = lanes(z, CH)
    mbc, ibc = to_col(vec[3:4, mine]), to_col(vec[5:6, mine])
    groups = [[0]] + [[2 * t - 1, 2 * t] for t in range(1, HALF)] + [[NZ - 1]]
    order = [0] + [x for t in range(1, HALF) for x in (t, NZ - t)] + [HALF]
    sib_of = {order[p]: g for g, ps in enumerate(groups) for p in ps}
    got = {}

    def to_sibling(m, s):
        at = (k, s, rows(zz(m), CH))
        n = sib_of[m % NZ] + (s if m % NZ == HALF else 0)
        send("sib", sh.at[at], sh.at[at], sibling, sib_sem.at[n])

    for s in range(NS):
        swap[s].wait_recv()
        tot = hy[s].astype(F32) + hyin[s].astype(F32)
        at_i = pl.ds(pl.multiple_of(k * HI + s * W, 128), W)
        mar, iar, cdr = vec[0:1, at_i], vec[2:3, at_i], vec[6:7, at_i]
        outer = ibc * iar
        corr = (tot * (1.0 / N) - mbc * mar) * outer
        slope = jnp.where(diag_mask(z, k, s), -2.0 * (1.0 - cdr), 2.0 * LAMBDA_OFF * corr)
        at = (k, s, rows(z, CH))
        sh[at] = (slope * outer).astype(BF16)
        for di in (R, L):
            got[1, di, s] = send("ag", sh.at[at], sh.at[at], at_z(SGN[di]), ag_sem.at[0, di, s])
        to_sibling(0, s)

    rtv[...] = jnp.zeros_like(rtv)
    sav[...] = jnp.zeros_like(sav)

    def piece(m, s):
        zc = zz(m)
        at = lanes(zc, CH)
        mbc, vbc = to_col(vec[3:4, at]), to_col(vec[4:5, at])
        ct = jnp.zeros((CH, W), F32)
        shift = jnp.zeros((CH, W), F32)
        for half in range(2):
            w = slice(half * HI + s * W, half * HI + (s + 1) * W)
            sf = sh[half, s, rows(zc, CH), :].astype(F32)
            q = jnp.where(diag_mask(zc, half, s), 0.0, sf * sf)
            ct = ct + q * vec[1:2, w]
            shift = shift + sf * vec[0:1, w]
            rtv[0:1, w] += jnp.sum(q * vbc, axis=0, keepdims=True)
            sav[0:1, w] += jnp.sum(sf * mbc, axis=0, keepdims=True)
        return ct, shift

    def chunk(m, slot, terms):
        zc = zz(m)
        at = lanes(zc, CH)
        mbr, vbr, ibr, cdc = vec[3:4, at], vec[4:5, at], vec[5:6, at], vec[6:7, at]
        ct, shift = terms[0]
        for c, v in terms[1:]:
            ct, shift = ct + c, shift + v
        ct = to_row(jnp.sum(ct, axis=1, keepdims=True)) * vbr * (0.5 / LAMBDA_OFF)
        shift = to_row(jnp.sum(shift, axis=1, keepdims=True))
        back = jnp.zeros((S, CH), F32)
        for half in range(2):
            sb = jnp.concatenate([sh[half, s, rows(zc, CH), :] for s in range(NS)], axis=1)
            back = back + lax.dot_general(a_ref[:, half * HI:(half + 1) * HI], sb, (((1,), (1,)), ((), ())),
                                          preferred_element_type=F32)
        ls[pl.ds(zc, 1), :] = ct
        ct = ct + diag_f * (-2.0 * (1.0 - cdc) * cdc)
        grad = back - shift - (ibr * ibr * ct) * (b_ref[:, at].astype(F32) - mbr)
        gb[slot] = grad.astype(BF16)

    PA, SH = S // NX, S // 2
    own_half, far_half = rows(row // 2, SH), rows(1 - row // 2, SH)
    out_at = [lanes(zz(m), CH) for m in order]
    other_end = {"row": (2 - row + NY) * (NY - 1) % NY}
    pair, cross, both, outs, give = [], [], [], [], []
    for p in range(NZ):
        n = NS + 4 * p
        pair.append([make("pair", gb.at[p, w], gbe.at[p, w], buddy, y_sem.at[n + 2 + i])
                     for i, w in enumerate((far_half, own_half))])
        cross.append(make("cross", gbs.at[p, far_half], gbm.at[p], other_mid, y_sem.at[n + 1]))
        both.append(make("both", gbt.at[p, own_half], gbt.at[p, own_half], other_mid, y_sem.at[n]))
        w = own_half if p >= NZ - 2 else far_half
        give.append([make("give", gbt.at[p, own_half], ob_ref.at[own_half, out_at[p]], buddy),
                     make("give", gbt.at[p, w], ob_ref.at[w, out_at[p]], other_end if p >= NZ - 2 else buddy)])
        outs.append(keep(gbt.at[p], ob_ref.at[:, out_at[p]], "mid"))

    def step1(p):
        @pl.when(is_end)
        def _():
            for c in pair[p]:
                c.start()

    def step2(*ps):
        @pl.when(is_mid)
        def _():
            for p in ps:
                pair[p][0].wait_recv()
                gbs[p, far_half, :] = (gb[p, far_half, :].astype(F32) + gbe[p, far_half, :].astype(F32)).astype(BF16)
                cross[p].start()

    def step3(*ps):
        @pl.when(is_mid)
        def _():
            for p in ps:
                pair[p][1].wait_recv()
                cross[p].wait_recv()
                v = gb[p, own_half, :].astype(F32) + gbe[p, own_half, :].astype(F32)
                gbt[p, own_half, :] = (v + gbm[p].astype(F32)).astype(BF16)
                both[p].start()
                give[p][0].start()
                if p >= NZ - 2:
                    give[p][1].start()

    def step4(*ps):
        @pl.when(is_mid)
        def _():
            for p in ps:
                both[p].wait_recv()
                if p < NZ - 2:
                    give[p][1].start()
                outs[p].start()

    def group_compute(g):
        got_all("sib", sh.at[0, :, pl.ds(0, len(groups[g]) * CH)], sib_sem.at[g])
        for p in groups[g]:
            chunk(order[p], p, [piece(order[p], s) for s in range(NS)])
            step1(p)

    def advance(g):
        for n, step in ((g - 1, step2), (g - 2, step3), (g - 3, step4)):
            if 0 <= n < len(groups):
                step(*groups[n])

    for t in range(1, HALF):
        for s in range(NS):
            for di in (R, L):
                got[t, di, s].wait_recv()
                m = (-SGN[di] * t) % NZ
                at = (k, s, rows(zz(m), CH))
                if t < HALF - 1 or s % 2 == di:
                    got[t + 1, di, s] = send("ag", sh.at[at], sh.at[at], at_z(SGN[di]), ag_sem.at[t, di, s])
                to_sibling(m, s)
        group_compute(t - 1)
        advance(t - 1)
    group_compute(HALF - 1)

    advance(HALF - 1)

    terms = []
    scat_sem = NS + 4 * NZ

    def last(s):
        got_all("sib", sh.at[0, s, pl.ds(0, CH)], sib_sem.at[HALF + s])
        terms.append(piece(HALF, s))

    def send_a(s):
        for half in range(2):
            w = slice(half * HI + s * W, half * HI + (s + 1) * W)
            mar, var, iar, cdr = vec[0:1, w], vec[1:2, w], vec[2:3, w], vec[6:7, w]
            acc = jnp.dot(b_ref[...], sh[half, s], preferred_element_type=F32)
            rt = rtv[0:1, w] * var * (0.5 / LAMBDA_OFF) + diag_f * (-2.0 * (1.0 - cdr) * cdr)
            grad = acc - sav[0:1, w] - (iar * iar * rt) * (a_ref[:, w].astype(F32) - mar)
            ga[s, :, half * W:(half + 1) * W] = grad.astype(BF16)
        for d in range(1, NX):
            send("scat", ga.at[s, rows((col + d) % NX, PA), :], gars.at[s, col], xs[d - 1], y_sem.at[scat_sem + s])

    def finish_a(s):
        got_all("scat", gars.at[s, pl.ds(0, NX - 1)], y_sem.at[scat_sem + s])
        v = ga[s, rows(col, PA), :].astype(F32)
        for d in range(1, NX):
            v = v + gars[s, (col + d) % NX].astype(F32)
        gat[s] = v.astype(BF16)
        for half in range(2):
            src = gat.at[s, :, pl.ds(half * W, W)]
            at = (rows(col, PA), pl.ds(half * HI + s * W, W))
            for dev in xs:
                send("gath", src, oa_ref.at[at], dev)
            keep(src, oa_ref.at[at]).start()

    for s in range(NS):
        got[HALF, s % 2, s].wait_recv()
        to_sibling(HALF, s)
        if s:
            last(s - 1)
            if s < NS - 1:
                send_a(s - 1)
    last(NS - 1)
    chunk(HALF, NZ - 1, terms)
    step1(NZ - 1)

    cdv = vec[6:7, :]
    part_loss = 0.5 * jnp.sum(jnp.sum(ls[...], axis=0, keepdims=True), axis=1, keepdims=True) + \
        diag_f * jnp.sum(jnp.square(1.0 - cdv), axis=1, keepdims=True)
    lx[col] = jnp.broadcast_to(part_loss, (8, 128))
    for dev in xs:
        send("lx", lx.at[col], lx.at[col], dev)
    step2(*groups[HALF - 1])
    for s in range(NS - 2, NS):
        send_a(s)
    step3(*groups[HALF - 2])
    step4(*groups[HALF - 3])
    step2(NZ - 1)
    step3(*groups[HALF - 1])
    finish_a(0)
    step4(*groups[HALF - 2])
    got_all("lx", lx.at[pl.ds(0, NX - 1)])
    v = lx[0]
    for n in range(1, NX):
        v = v + lx[n]
    ly[row] = v
    for dev in ys:
        send("ly", ly.at[row], ly.at[row], dev)
    finish_a(1)
    step3(NZ - 1)
    finish_a(2)
    step4(*groups[HALF - 1])
    finish_a(3)
    step4(NZ - 1)

    got_all("ly", ly.at[pl.ds(0, NY - 1)])
    v = ly[0]
    for n in range(1, NY):
        v = v + ly[n]
    loss_ref[0, 0] = v[0, 0] / FEAT

    for c in (get_b, get_a, st1, st3):
        c.wait_send()
    for name, ref in (("b", bx.at[:, pl.ds(0, F - CH)]), ("st2", st_rs.at[pl.ds(0, NZ - 1)]), ("st4", st_rs.at[pl.ds(0, NZ - 1)]),
                      ("rs", sh.at[0, :, pl.ds(0, (NZ - 1) * CH)]), ("swap", hy),
                      ("ag", sh.at[0, :, pl.ds(0, (NZ - 1) * CH)]), ("sib", sh.at[0]),
                      ("scat", gars.at[:, pl.ds(0, NX - 1)]), ("gath", gars.at[:, pl.ds(0, NX - 1)]),
                      ("lx", lx.at[pl.ds(0, NX - 1)]), ("ly", ly.at[pl.ds(0, NY - 1)])):
        sent_all(name, ref)

    @pl.when(is_end)
    def _():
        got_all("give", gbt)
        sent_all("pair", gb)

    @pl.when(is_mid)
    def _():
        sent_all("cross", gbm)
        sent_all("both", gbm)
        sent_all("give", gbt)
        for c, r in local:
            if r == "mid":
                c.wait()

    got_all("gath", gars.at[:, pl.ds(0, NX - 1)])
    for c, r in local[2:]:
        if r is None:
            c.wait()
    assert len(local) <= NLOC


def build(mesh, NZ, YH, samples, feat):
    NX, NY = mesh.shape["col"], mesh.shape["row"]

    def on_device(a, b):
        S, F = a.shape
        CH, HI, W, HALF = F // NZ, F // 2, F // 2 // NS, NZ // 2
        cfg = (NZ, YH, NX, NY, S, F, samples, feat)
        hbm = pl.BlockSpec(memory_space=pl.ANY)
        V = pltpu.VMEM
        ga, gb, loss = pl.pallas_call(
            functools.partial(kernel, cfg),
            out_shape=(jax.ShapeDtypeStruct((S, F), BF16), jax.ShapeDtypeStruct((S, F), BF16),
                       jax.ShapeDtypeStruct((1, 1), F32)),
            in_specs=[pl.BlockSpec(memory_space=pltpu.HBM)] * 2,
            out_specs=(hbm, hbm, pl.BlockSpec(memory_space=pltpu.SMEM)),
            scratch_shapes=[
                V((S, F), BF16), V((S, F), BF16), V((S, HI), BF16), V((S, F), BF16),
                V((8, F), F32), V((8, F), F32), V((8, F), F32), V((NZ, 8, CH), F32), V((8, CH), F32),
                V((8, CH), F32), V((8, F), F32), V((8, F), F32),
                V((NZ, CH, HI), F32), V((HALF, 2, NS, CH, W), BF16), V((NS, CH, W), BF16),
                V((NS, CH, W), BF16), V((NS, CH, W), BF16), V((2, NS, F, W), BF16),
                V((NZ, S, CH), BF16), V((NZ, S, CH), BF16), V((NZ, S, CH), BF16), V((NZ, S // 2, CH), BF16),
                V((NZ, S, CH), BF16),
                V((NS, S, 2 * W), BF16), V((NS, NX, S // NX, 2 * W), BF16), V((NS, S // NX, 2 * W), BF16),
                V((8, F), F32), V((8, F), F32), V((NZ, CH), F32), V((NX, 8, 128), F32), V((NY, 8, 128), F32),
                pltpu.SemaphoreType.DMA((19,)), pltpu.SemaphoreType.DMA((19,)),
                pltpu.SemaphoreType.DMA((HALF, 2, NS)), pltpu.SemaphoreType.DMA((HALF, 2, NS)),
                pltpu.SemaphoreType.DMA((HALF + NS,)), pltpu.SemaphoreType.DMA((2 * NS + 4 * NZ,)),
                pltpu.SemaphoreType.DMA((NLOC,)),
            ],
            compiler_params=pltpu.CompilerParams(collective_id=0, has_side_effects=True,
                                                 vmem_limit_bytes=53 * 1024 * 1024),
            name="twins",
        )(a, b)
        return ga.astype(F32), gb.astype(F32), loss.reshape(())

    placed = (P("batch", "row"), P("batch", "col"))
    return jax.shard_map(on_device, mesh=mesh, in_specs=placed, out_specs=placed + (P(),), check_vma=False)


def solution(mesh):
    return build(mesh, 8, 2, 8192, 4096)
```
